512 devices in a mesh: dp: 64 (over z, x_hi, core), rep: 8 (over y, x_lo).
Axes of the slice: x: 4 (x_hi: 2, x_lo: 2; x = x_hi * 2 + x_lo), y: 4, z: 16, core: 2. Of those that a mesh axis runs over, the one named last changes fastest.
Arguments:
- grad_out: bfloat16 [49152, 2048], P('dp', 'rep'), may hold values from -16 to 16
- pre_act: bfloat16 [49152, 3072], P('dp', 'rep'), may hold values from -6 to 6
- up_weight: bfloat16 [3072, 2048], P('rep'), may hold values from -0.125 to 0.125
- down_weight: bfloat16 [2048, 3072], P(None, 'rep'), may hold values from -0.109375 to 0.109375
- slot_counts: int32 [64], P('dp'), may hold values from 384 to 768, as said below
Outputs:
- input_grad: bfloat16 [49152, 2048], P('dp')
- down_grad: float32 [2048, 3072], P('dp', 'rep')
The draws below stay inside these ranges and needn't reach their ends.
Inputs may be any that keep to these rules, and one draw needn't show every extreme that they name: Row i * 768 + j is live exactly when j < slot_counts[i]; some index has all 768 slots live and some index exactly 384.
All inputs are finite; a program needn't handle non-finite values.
Results may differ from the reference program's by a relative error of at most 0.0049.
Values may be sent and summed in bfloat16 or wider, within the bound.
No kernel may reach another device: no remote copies, remote signals or barrier semaphores. Data moves between devices by JAX's collectives and lax.ppermute only.
A program may use at most 64 MiB of HBM per device.

```python
import jax
import jax.numpy as jnp
from jax import lax

D = 2048
FF = 3072
CAP = 768
ROWS = 49152
N_DP = 64


def draw_slot_counts(key, part):
    counts = jax.random.randint(key, (N_DP,), CAP // 2, CAP + 1)
    fullest = jax.random.randint(jax.random.fold_in(key, 1), (), 0, N_DP)
    step_away = jax.random.randint(jax.random.fold_in(key, 2), (), 1, max(N_DP, 2))
    emptiest = (fullest + step_away) % N_DP
    counts = counts.at[emptiest].set(CAP // 2)
    counts = counts.at[fullest].set(CAP)
    return counts.astype(jnp.int32)


def with_spikes(values, rng, source, target, shards_of, factor):
    def block_of(axis_at):
        return (jnp.arange(values.shape[axis_at]) // (values.shape[axis_at] // shards_of)).reshape((-1,) + (1,) * (values.ndim - 1 - axis_at))

    near = jax.random.permutation(rng, shards_of)[block_of(target)]
    other_side = (block_of(target) + shards_of // 2) % shards_of
    return jnp.where((block_of(source) == near) | (block_of(source) == other_side), factor * values, values)


def shard_levels(key, shape, cuts, smallest, high):
    def one(axis_at, parts):
        heights = jax.random.uniform(jax.random.fold_in(jax.random.fold_in(key, 6), axis_at), (parts,), jnp.float32, smallest / len(cuts), high / len(cuts))
        return jnp.repeat(jnp.exp(heights), shape[axis_at] // parts).reshape((-1,) + (1,) * (len(shape) - axis_at - 1))

    loudness = one(*cuts[0])
    for cut in cuts[1:]:
        loudness = loudness * one(*cut)
    return loudness


def normal_values(own_key, shape, deviation, most, cuts=(), kind=jnp.bfloat16):
    drawn = deviation * jax.random.normal(own_key, shape, jnp.float32)
    if cuts:
        drawn = drawn * shard_levels(own_key, shape, cuts, -0.22, 0.18)
    return jnp.clip(drawn, -most, most).astype(kind)


def noise_with(own_key, extent, width, limit, shards, heavy, dtype=jnp.bfloat16):
    entries = width * jax.random.normal(own_key, extent, jnp.float32)
    if shards:
        entries = entries * shard_levels(own_key, extent, shards, -0.22, 0.18)
    return jnp.clip(with_spikes(entries, jax.random.fold_in(own_key, 3), *heavy), -limit, limit).astype(dtype)


def setup_inputs(seed: int = 0) -> dict:
    splits = jax.random.split(jax.random.key(seed), 6)
    grad_out = noise_with(splits[0], (ROWS, D), 1.0, 16.0, ((0, 64), (1, 8)), (0, 1, 64, 4.0))
    pre_act = normal_values(splits[1], (ROWS, FF), 1.0, 6.0, ((0, 64), (1, 8)))
    up_weight = normal_values(splits[2], (FF, D), D ** -0.5, 0.125, ((0, 8),))
    down_weight = normal_values(splits[3], (D, FF), FF ** -0.5, 0.109375, ((1, 8),))
    slot_counts = draw_slot_counts(jax.random.fold_in(splits[5], 71), 0)
    return {"grad_out": grad_out, "pre_act": pre_act, "up_weight": up_weight, "down_weight": down_weight, "slot_counts": slot_counts}


def reference(grad_out, pre_act, up_weight, down_weight, slot_counts):
    row_index = lax.iota(jnp.int32, N_DP * CAP)
    live_rows = ((row_index % CAP) < slot_counts[row_index // CAP])[:, None]
    grad_live = jnp.where(live_rows, grad_out, jnp.zeros_like(grad_out))
    zero_pre = jnp.zeros_like(pre_act)
    hidden = jnp.where(live_rows, jnp.maximum(pre_act, zero_pre), zero_pre)
    down_grad = jnp.dot(grad_live.T, hidden, preferred_element_type=jnp.float32) / N_DP
    hidden_grad = jnp.dot(grad_live, down_weight, preferred_element_type=jnp.float32)
    pre_grad = jnp.where(pre_act > 0, hidden_grad, jnp.zeros_like(hidden_grad)).astype(jnp.bfloat16)
    input_grad = jnp.dot(pre_grad, up_weight, preferred_element_type=jnp.float32).astype(jnp.bfloat16)
    return input_grad, down_grad
```

```python
import jax
import jax.numpy as jnp
from jax import lax
from jax.sharding import Mesh
from jax.sharding import PartitionSpec as P

DP = ("z", "xh", "core")
REP = ("y", "xl")
PAIR = [(0, 1), (1, 0)]


def to_all(block, axes, ranks):
    copies = jnp.broadcast_to(block[None], (ranks, *block.shape))
    return lax.all_to_all(copies, axes, 0, 0, tiled=True)


def on_device(grad_out, pre_act, up_weight, down_weight, slot_counts):
    slot_rows, features = grad_out.shape
    hidden_units = pre_act.shape[1]
    reps = lax.axis_size(REP)
    data_ranks = lax.axis_size(DP)
    model_width = features * reps
    live_rows = (lax.iota(jnp.int32, slot_rows) < slot_counts[0])[:, None]
    grad_live = jnp.where(live_rows, grad_out, jnp.zeros_like(grad_out))
    zero_pre = jnp.zeros_like(pre_act)
    hidden = jnp.where(live_rows, jnp.maximum(pre_act, zero_pre), zero_pre)

    grads = to_all(grad_live, REP, reps)

    weights = down_weight.reshape(reps, features, hidden_units)
    hidden_grad = sum(
        jnp.dot(grads[j], weights[j], preferred_element_type=jnp.float32) for j in range(reps)
    )
    pre_grad = jnp.where(pre_act > 0, hidden_grad, 0.0).astype(jnp.bfloat16)
    terms = jnp.dot(pre_grad, up_weight, preferred_element_type=jnp.float32).astype(jnp.bfloat16)
    terms = lax.all_to_all(terms, REP, 0, 0, tiled=True)
    terms = terms.reshape(reps, slot_rows // reps, model_width)
    own_rows = jnp.sum(terms.astype(jnp.float32), axis=0).astype(jnp.bfloat16)
    input_grad = to_all(own_rows, REP, reps).reshape(slot_rows, model_width)

    down_terms = lax.dot_general(
        grads, hidden, (((1,), (0,)), ((), ())), preferred_element_type=jnp.float32
    ).astype(jnp.bfloat16)
    share = model_width // data_ranks
    down_terms = down_terms.reshape(data_ranks // 2, 2, share, hidden_units)
    core = lax.axis_index("core")
    kept = lax.dynamic_index_in_dim(down_terms, core, 1, keepdims=False)
    sent = lax.dynamic_index_in_dim(down_terms, 1 - core, 1, keepdims=False)
    came = lax.ppermute(sent, "core", PAIR)
    chip_terms = kept.astype(jnp.float32) + came.astype(jnp.float32)
    z_terms = chip_terms.reshape(-1, hidden_units)
    z_sum = lax.psum_scatter(z_terms, "z", scatter_dimension=0, tiled=True)
    z_sum = z_sum.reshape(2, share, hidden_units)
    xh = lax.axis_index("xh")
    kept = lax.dynamic_index_in_dim(z_sum, xh, 0, keepdims=False)
    sent = lax.dynamic_index_in_dim(z_sum, 1 - xh, 0, keepdims=False)
    down_grad = (kept + lax.ppermute(sent, "xh", PAIR)) / data_ranks
    return (input_grad, down_grad)


def solution(mesh):
    z_ranks = mesh.shape["dp"] // 4
    y_ranks = mesh.shape["rep"] // 2
    finer = Mesh(mesh.devices.reshape(z_ranks, 2, 2, y_ranks, 2), (*DP, *REP))
    in_specs = (P(DP, REP), P(DP, REP), P(REP, None), P(None, REP), P(DP))
    out_specs = (P(DP, None), P(DP, REP))
    return jax.shard_map(
        on_device, mesh=finer, in_specs=in_specs, out_specs=out_specs, check_vma=False
    )
```

```python
import jax
import jax.numpy as jnp
from jax import lax
from jax.experimental import pallas as pl
from jax.experimental.pallas import tpu as pltpu
from jax.sharding import Mesh
from jax.sharding import PartitionSpec as P

DP = ("z", "xh", "core")
REP = ("y", "xl")
RING = ("xh", "xl")
NEAR = [(0, 1), (1, 0)]
FAR = [(0, 3), (3, 0), (1, 2), (2, 1)]
ACROSS = [(0, 2), (2, 0), (1, 3), (3, 1)]
VMEM = pl.BlockSpec(memory_space=pltpu.VMEM)
SMEM = pl.BlockSpec(memory_space=pltpu.SMEM)
ANY = pl.BlockSpec(memory_space=pl.ANY)
LIMIT = 40 * 1024 * 1024


def dot(a, b):
    return jnp.dot(a, b, preferred_element_type=jnp.float32)


def terms_kernel(place, grads, pre_own, pre_far, down_own, down_mine, down_other, up_own, up_mine, up_other, terms):
    core = place[0]
    blocks, features = grads.shape[0], grads.shape[2]
    half = blocks // 2
    own = sum(dot(grads[j], down_own[j * features:(j + 1) * features, :]) for j in range(blocks))
    far = sum(
        dot(grads[core * half + j], down_mine[j * features:(j + 1) * features, :]) for j in range(half)
    ) + sum(
        dot(grads[(1 - core) * half + j], down_other[j * features:(j + 1) * features, :]) for j in range(half)
    )
    own = jnp.where(pre_own[...] > 0, own, 0.0).astype(jnp.bfloat16)
    far = jnp.where(pre_far[...] > 0, far, 0.0).astype(jnp.bfloat16)
    columns = up_mine.shape[1]
    for up_part, start in ((up_mine, core * columns), (up_other, (1 - core) * columns)):
        at = pl.ds(pl.multiple_of(start, columns), columns)
        terms[:, at] = (dot(own, up_own[:, at]) + dot(far, up_part[...])).astype(terms.dtype)


def down_kernel(place, grads, pre_own, pre_far, kept, sent):
    core, xh, xl, live = place[0], place[1], place[2], place[3]
    blocks, rows, features = grads.shape
    share = kept.shape[2]
    groups = features // (4 * share)
    at = lax.broadcasted_iota(jnp.int32, pre_own.shape, 0)
    part = rows // 4
    row = at + (at // part + xl) * part
    for t, pre in ((0, pre_own), (1, pre_far)):
        hidden = jnp.where(row < live, jnp.maximum(pre[...], 0), 0).astype(jnp.bfloat16)
        for j in range(blocks):
            block = lax.dot_general(
                grads[j], hidden, (((0,), (0,)), ((), ())), preferred_element_type=jnp.float32
            ).astype(kept.dtype)
            for g in range(groups):
                z = j * groups + g
                for h in range(2):
                    first = (g * 4 + h * 2) * share
                    kind = t * 2 + jnp.abs(xh - h)
                    low = block[first:first + share, :]
                    high = block[first + share:first + 2 * share, :]

                    @pl.when(core == 0)
                    def _():
                        kept[kind, z] = low
                        sent[kind, z] = high

                    @pl.when(core != 0)
                    def _():
                        kept[kind, z] = high
                        sent[kind, z] = low


def place_kernel(place, own, near, below, above, far_low, far_high, near_below, near_above, near_far, out, sems):
    y, xl = place[4], place[2]
    rows = own.shape[0]
    half = rows // 2
    ranks = out.shape[0] // (2 * rows)

    def start(dy, dx, offset):
        at = ((y + dy) % ranks) * 2 + (1 - xl if dx else xl)
        return pl.multiple_of(at * rows + offset, 16)

    copies = [
        (own, 0, 0, 0), (near, 0, 1, 0), (below, ranks - 1, 0, 0), (above, 1, 0, 0),
        (far_low, 2, 0, 0), (far_high, 2, 0, half),
        (near_below, ranks - 1, 1, 0), (near_above, 1, 1, 0), (near_far, 2, 1, 0),
    ]
    running = []
    for i, (block, dy, dx, offset) in enumerate(copies):
        copy = pltpu.make_async_copy(
            block, out.at[pl.ds(start(dy, dx, offset), block.shape[0])], sems.at[i]
        )
        copy.start()
        running.append(copy)
    for copy in running:
        copy.wait()


def own_part(array, index, axis):
    return lax.dynamic_index_in_dim(array, index, axis, keepdims=False)


def on_device(grad_out, pre_act, up_weight, down_weight, slot_counts):
    slot_rows, features = grad_out.shape
    hidden_units = pre_act.shape[1]
    ys, zs = lax.axis_size("y"), lax.axis_size("z")
    reps = 2 * ys
    width = features * reps
    rows = slot_rows // reps
    half_rows = slot_rows // 2
    core, xh, xl, y = (lax.axis_index(a) for a in ("core", "xh", "xl", "y"))
    place = jnp.stack([core, xh, xl, slot_counts[0], y]).astype(jnp.int32)
    bf16 = jnp.bfloat16

    def turn(by):
        return [(i, (i + by) % ys) for i in range(ys)]

    live_rows = (lax.iota(jnp.int32, slot_rows) < slot_counts[0])[:, None]
    grad_live = jnp.where(live_rows, grad_out, jnp.zeros_like(grad_out))
    by_set = grad_live.reshape(ys, 2, rows, features).transpose(1, 0, 2, 3).reshape(2, half_rows, features)
    grads = jnp.broadcast_to(by_set[None], (ys, 2, half_rows, features)).reshape(reps, half_rows, features)
    grads = lax.all_to_all(grads, REP, 0, 0, tiled=True)

    pre_sets = pre_act.reshape(ys, 2, rows, hidden_units)
    pre_own = own_part(pre_sets, xl, 1).reshape(half_rows, hidden_units)
    pre_far = lax.ppermute(own_part(pre_sets, 1 - xl, 1).reshape(half_rows, hidden_units), "xl", NEAR)

    down_mine = lax.ppermute(own_part(down_weight.reshape(2, width // 2, hidden_units), core, 0), RING, FAR)
    up_mine = lax.ppermute(
        lax.dynamic_slice_in_dim(up_weight, core * (width // 2), width // 2, 1), RING, FAR
    )
    down_other = lax.ppermute(down_mine, "core", NEAR)
    up_other = lax.ppermute(up_mine, "core", NEAR)

    terms = pl.pallas_call(
        terms_kernel,
        out_shape=jax.ShapeDtypeStruct((half_rows, width), bf16),
        in_specs=[SMEM] + [VMEM] * 9,
        out_specs=VMEM,
        compiler_params=pltpu.CompilerParams(vmem_limit_bytes=LIMIT),
        cost_estimate=pl.CostEstimate(
            flops=8 * half_rows * width * hidden_units, bytes_accessed=16 * width * hidden_units, transcendentals=0
        ),
        name="terms",
    )(place, grads, pre_own, pre_far, down_weight, down_mine, down_other, up_weight, up_mine, up_other)

    share = width // (4 * zs)
    laid_out = jax.ShapeDtypeStruct((4, zs, share, hidden_units), bf16)
    kept, sent = pl.pallas_call(
        down_kernel,
        out_shape=(laid_out, laid_out),
        in_specs=[SMEM] + [VMEM] * 3,
        out_specs=(VMEM, VMEM),
        compiler_params=pltpu.CompilerParams(vmem_limit_bytes=LIMIT),
        cost_estimate=pl.CostEstimate(
            flops=4 * half_rows * width * hidden_units, bytes_accessed=8 * width * hidden_units, transcendentals=0
        ),
        name="down_terms",
    )(place, grads, pre_own, pre_far)

    came = lax.all_to_all(terms.reshape(ys, rows, width), "y", 0, 0, tiled=True)
    f32 = jnp.float32
    own = sum(came[i].astype(f32) for i in range(ys)).astype(bf16)

    other = lax.ppermute(sent, "core", NEAR)
    chip = [(kept[k].astype(f32) + other[k].astype(f32)) for k in range(4)]
    ring = [
        lax.ppermute(chip[2].astype(bf16), "xl", NEAR),
        lax.ppermute(chip[1].astype(bf16), RING, ACROSS),
        lax.ppermute(chip[3].astype(bf16), RING, FAR),
    ]
    ring_sum = (chip[0] + sum(part.astype(f32) for part in ring)).astype(bf16)
    z_terms = lax.all_to_all(ring_sum, "z", 0, 0, tiled=True)
    down_grad = jnp.sum(z_terms.astype(f32), axis=0) / (4 * zs)

    near = lax.ppermute(own, "xl", NEAR)
    below = lax.ppermute(own, "y", turn(1))
    above = lax.ppermute(own, "y", turn(-1))
    far_low = lax.ppermute(below[:rows // 2], "y", turn(1))
    far_high = lax.ppermute(above[rows // 2:], "y", turn(-1))
    near_below = lax.ppermute(below, "xl", NEAR)
    near_above = lax.ppermute(above, "xl", NEAR)
    near_far = lax.ppermute(near, "y", turn(2))
    input_grad = pl.pallas_call(
        place_kernel,
        out_shape=jax.ShapeDtypeStruct((slot_rows, width), bf16),
        in_specs=[SMEM] + [ANY] * 9,
        out_specs=ANY,
        scratch_shapes=[pltpu.SemaphoreType.DMA((9,))],
        name="place",
    )(place, own, near, below, above, far_low, far_high, near_below, near_above, near_far)
    return (input_grad, down_grad)


def solution(mesh):
    zs = mesh.shape["dp"] // 4
    ys = mesh.shape["rep"] // 2
    finer = Mesh(mesh.devices.reshape(zs, 2, 2, ys, 2), (*DP, *REP))
    in_specs = (P(DP, REP), P(DP, REP), P(REP, None), P(None, REP), P(DP))
    out_specs = (P(DP, None), P(DP, REP))
    return jax.shard_map(
        on_device, mesh=finer, in_specs=in_specs, out_specs=out_specs, check_vma=False
    )
```

```python
import jax
import jax.numpy as jnp
from jax import lax
from jax.experimental import pallas as pl
from jax.experimental.pallas import tpu as pltpu
from jax.sharding import Mesh
from jax.sharding import PartitionSpec as P

DP = ("z", "xh", "core")
REP = ("y", "xl")
RING = ("xh", "xl")
NEAR = [(0, 1), (1, 0)]
FAR = [(0, 3), (3, 0), (1, 2), (2, 1)]
MIXED = [(i, i ^ 1 if i // 2 % 2 == 0 else i ^ 5) for i in range(8)]
ACROSS = [(0, 2), (2, 0), (1, 3), (3, 1)]
VMEM = pl.BlockSpec(memory_space=pltpu.VMEM)
SMEM = pl.BlockSpec(memory_space=pltpu.SMEM)
ANY = pl.BlockSpec(memory_space=pl.ANY)
LIMIT = 40 * 1024 * 1024


def dot(a, b):
    return jnp.dot(a, b, preferred_element_type=jnp.float32)


def own_kernel(grads, pre, down, out):
    blocks, _, features = grads.shape
    hidden = sum(dot(grads[j], down[j * features:(j + 1) * features, :]) for j in range(blocks))
    out[...] = jnp.where(pre[...] > 0, hidden, 0.0).astype(out.dtype)


def terms_kernel(place, grads, own, pre_far, down_mine, down_other, up_own, up_mine, up_other, terms, up_far):
    core = place[0]
    blocks, features = grads.shape[0], grads.shape[2]
    half = blocks // 2
    units = up_mine.shape[0]
    up_far[pl.ds(pl.multiple_of(core * units, 16), units), :] = up_mine[...]
    up_far[pl.ds(pl.multiple_of((1 - core) * units, 16), units), :] = up_other[...]
    far = sum(
        dot(grads[core * half + j], down_mine[j * features:(j + 1) * features, :]) for j in range(half)
    ) + sum(
        dot(grads[(1 - core) * half + j], down_other[j * features:(j + 1) * features, :]) for j in range(half)
    )
    far = jnp.where(pre_far[...] > 0, far, 0.0).astype(jnp.bfloat16)
    terms[...] = (dot(own[...], up_own[...]) + dot(far, up_far[...])).astype(terms.dtype)


def down_kernel(place, grads, pre_own, pre_far, kept, sent):
    core, xh, xl, live = place[0], place[1], place[2], place[3]
    blocks, rows, features = grads.shape
    units = pre_own.shape[1]
    share = kept.shape[2]
    groups = features // (4 * share)
    at = lax.broadcasted_iota(jnp.int32, pre_own.shape, 0)
    part = rows // 4
    row = at + (at // part + xl) * part
    hidden = jnp.concatenate(
        [jnp.where(row < live, jnp.maximum(pre[...], 0), 0).astype(jnp.bfloat16) for pre in (pre_own, pre_far)],
        axis=1,
    )
    for j in range(blocks):
        block = lax.dot_general(
            grads[j], hidden, (((0,), (0,)), ((), ())), preferred_element_type=jnp.float32
        ).astype(kept.dtype)
        for g in range(groups):
            z = j * groups + g
            for h in range(2):
                first = (g * 4 + h * 2) * share
                low = block[first:first + share, :]
                high = block[first + share:first + 2 * share, :]
                mine = jnp.where(core == 0, low, high)
                other = jnp.where(core == 0, high, low)
                for t in range(2):
                    kind = t * 2 + jnp.abs(xh - h)
                    kept[kind, z] = mine[:, t * units:(t + 1) * units]
                    sent[kind, z] = other[:, t * units:(t + 1) * units]


def put(place, blocks, out, sems):
    y, xl = place[4], place[2]
    rows = blocks[0][0].shape[0] if len(blocks[0]) == 3 else blocks[0][4]
    ranks = out.shape[0] // (2 * rows)
    running = []
    for i, (block, dy, dx, *rest) in enumerate(blocks):
        at = ((y + dy + ranks) % ranks) * 2 + (1 - xl if dx else xl)
        start = pl.multiple_of(at * rows, 16)
        source = block.at[pl.ds(rest[0], rows)] if rest else block
        copy = pltpu.make_async_copy(source, out.at[pl.ds(start, rows)], sems.at[i])
        copy.start()
        running.append(copy)
    for copy in running:
        copy.wait()


def first_kernel(place, own, near, below, above, out, sems):
    put(place, [(own, 0, 0), (near, 0, 1), (below, -1, 0), (above, 1, 0)], out, sems)


def last_kernel(place, partial, across, beside, out, sems):
    rows = across.shape[0] // 2
    put(
        place,
        [(across, 2, 0, 0, rows), (across, 2, 1, rows, rows), (beside, -1, 1, 0, rows), (beside, 1, 1, rows, rows)],
        out,
        sems,
    )


def own_part(array, index, axis):
    return lax.dynamic_index_in_dim(array, index, axis, keepdims=False)


def on_device(grad_out, pre_act, up_weight, down_weight, slot_counts):
    slot_rows, features = grad_out.shape
    hidden_units = pre_act.shape[1]
    ys, zs = lax.axis_size("y"), lax.axis_size("z")
    reps = 2 * ys
    width = features * reps
    rows = slot_rows // reps
    half_rows = slot_rows // 2
    core, xh, xl, y = (lax.axis_index(a) for a in ("core", "xh", "xl", "y"))
    place = jnp.stack([core, xh, xl, slot_counts[0], y]).astype(jnp.int32)
    bf16 = jnp.bfloat16

    def turn(by):
        return [(i, (i + by) % ys) for i in range(ys)]

    live_rows = (lax.iota(jnp.int32, slot_rows) < slot_counts[0])[:, None]
    grad_live = jnp.where(live_rows, grad_out, jnp.zeros_like(grad_out))
    by_set = grad_live.reshape(ys, 2, rows, features).transpose(1, 0, 2, 3).reshape(2, half_rows, features)
    grads = jnp.broadcast_to(by_set[None], (ys, 2, half_rows, features)).reshape(reps, half_rows, features)
    grads = lax.all_to_all(grads, REP, 0, 0, tiled=True)

    pre_sets = pre_act.reshape(ys, 2, rows, hidden_units)
    pre_own = own_part(pre_sets, xl, 1).reshape(half_rows, hidden_units)
    pre_far = lax.ppermute(own_part(pre_sets, 1 - xl, 1).reshape(half_rows, hidden_units), "xl", NEAR)

    down_mine = lax.ppermute(own_part(down_weight.reshape(2, width // 2, hidden_units), core, 0), RING, FAR)
    up_mine = lax.ppermute(
        own_part(up_weight.reshape(2, hidden_units // 2, width), core, 0), ("xh", "core", "xl"), MIXED
    )
    down_other = lax.ppermute(down_mine, "core", NEAR)
    up_other = lax.ppermute(up_mine, "core", NEAR)

    pre_grad = pl.pallas_call(
        own_kernel,
        out_shape=jax.ShapeDtypeStruct((half_rows, hidden_units), bf16),
        in_specs=[VMEM] * 3,
        out_specs=VMEM,
        compiler_params=pltpu.CompilerParams(vmem_limit_bytes=LIMIT),
        cost_estimate=pl.CostEstimate(
            flops=2 * half_rows * width * hidden_units, bytes_accessed=4 * width * hidden_units, transcendentals=0
        ),
        name="own_grad",
    )(grads, pre_own, down_weight)
    terms = pl.pallas_call(
        terms_kernel,
        out_shape=jax.ShapeDtypeStruct((half_rows, width), bf16),
        in_specs=[SMEM] + [VMEM] * 8,
        out_specs=VMEM,
        scratch_shapes=[pltpu.VMEM((hidden_units, width), bf16)],
        compiler_params=pltpu.CompilerParams(vmem_limit_bytes=LIMIT),
        cost_estimate=pl.CostEstimate(
            flops=6 * half_rows * width * hidden_units, bytes_accessed=12 * width * hidden_units, transcendentals=0
        ),
        name="terms",
    )(place, grads, pre_grad, pre_far, down_mine, down_other, up_weight, up_mine, up_other)

    share = width // (4 * zs)
    laid_out = jax.ShapeDtypeStruct((4, zs, share, hidden_units), bf16)
    kept, sent = pl.pallas_call(
        down_kernel,
        out_shape=(laid_out, laid_out),
        in_specs=[SMEM] + [VMEM] * 3,
        out_specs=(VMEM, VMEM),
        compiler_params=pltpu.CompilerParams(vmem_limit_bytes=LIMIT),
        cost_estimate=pl.CostEstimate(
            flops=4 * half_rows * width * hidden_units, bytes_accessed=8 * width * hidden_units, transcendentals=0
        ),
        name="down_terms",
    )(place, grads, pre_own, pre_far)

    f32 = jnp.float32
    came = lax.all_to_all(terms.reshape(ys, rows, width), "y", 0, 0, tiled=True)
    own = sum(came[i].astype(f32) for i in range(ys)).astype(bf16)

    other = lax.ppermute(sent, "core", NEAR)
    chip = [(kept[k].astype(f32) + other[k].astype(f32)) for k in range(4)]
    ring = [
        lax.ppermute(chip[2].astype(bf16), "xl", NEAR),
        lax.ppermute(chip[3].astype(bf16), RING, FAR),
        lax.ppermute(chip[1].astype(bf16), RING, ACROSS),
    ]

    near = lax.ppermute(own, "xl", NEAR)
    below = lax.ppermute(own, "y", turn(1))
    above = lax.ppermute(own, "y", turn(-1))

    own_chip, ring, _ = lax.optimization_barrier((chip[0].astype(bf16), ring, own))
    ring_sum = (own_chip.astype(f32) + sum(part.astype(f32) for part in ring)).astype(bf16)
    z_terms = lax.all_to_all(ring_sum, "z", 0, 0, tiled=True)
    down_grad = jnp.sum(z_terms.astype(f32), axis=0) / (4 * zs)

    across = lax.ppermute(jnp.concatenate([own, near]), "y", turn(2))
    beside = lax.ppermute(jnp.concatenate([below, above]), "xl", NEAR)
    whole = jax.ShapeDtypeStruct((slot_rows, width), bf16)
    params = pltpu.CompilerParams(vmem_limit_bytes=LIMIT)
    first = pl.pallas_call(
        first_kernel,
        out_shape=whole,
        in_specs=[SMEM] + [VMEM] * 4,
        out_specs=ANY,
        scratch_shapes=[pltpu.SemaphoreType.DMA((4,))],
        compiler_params=params,
        name="place_first",
    )(place, own, near, below, above)
    input_grad = pl.pallas_call(
        last_kernel,
        out_shape=whole,
        in_specs=[SMEM, ANY] + [VMEM] * 2,
        out_specs=ANY,
        scratch_shapes=[pltpu.SemaphoreType.DMA((4,))],
        input_output_aliases={1: 0},
        compiler_params=params,
        name="place_last",
    )(place, first, across, beside)
    return (input_grad, down_grad)


def solution(mesh):
    zs = mesh.shape["dp"] // 4
    ys = mesh.shape["rep"] // 2
    finer = Mesh(mesh.devices.reshape(zs, 2, 2, ys, 2), (*DP, *REP))
    in_specs = (P(DP, REP), P(DP, REP), P(REP, None), P(None, REP), P(DP))
    out_specs = (P(DP, None), P(DP, REP))
    return jax.shard_map(
        on_device, mesh=finer, in_specs=in_specs, out_specs=out_specs, check_vma=False
    )
```

```python
import jax
import jax.numpy as jnp
from jax import lax
from jax.experimental import pallas as pl
from jax.experimental.pallas import tpu as pltpu
from jax.sharding import Mesh
from jax.sharding import PartitionSpec as P

DP = ("z", "xh", "core")
REP = ("y", "xl")
RING = ("xh", "xl")
NEAR = [(0, 1), (1, 0)]
FAR = [(0, 3), (3, 0), (1, 2), (2, 1)]
MIXED = [(i, i ^ 1 if i // 2 % 2 == 0 else i ^ 5) for i in range(8)]
ACROSS = [(0, 2), (2, 0), (1, 3), (3, 1)]
VMEM = pl.BlockSpec(memory_space=pltpu.VMEM)
SMEM = pl.BlockSpec(memory_space=pltpu.SMEM)
ANY = pl.BlockSpec(memory_space=pl.ANY)
LIMIT = 40 * 1024 * 1024


def dot(a, b):
    return jnp.dot(a, b, preferred_element_type=jnp.float32)


def split_kernel(place, grad_out, pre_act, own_set, other_set, pre_own, pre_sent):
    xl, live = place[2], place[3]
    part = own_set.shape[0] // 4
    for y in range(4):
        to = slice(y * part, (y + 1) * part)
        for x, grads, pre in ((xl, own_set, pre_own), (1 - xl, other_set, pre_sent)):
            first = pl.multiple_of((y * 2 + x) * part, 16)
            at = pl.ds(first, part)
            row = first + lax.broadcasted_iota(jnp.int32, (part, grads.shape[1]), 0)
            grads[to, :] = jnp.where(row < live, grad_out[at, :], 0).astype(grads.dtype)
            pre[to, :] = pre_act[at, :]


def spread_kernel(place, own_set, near_set, out):
    xl = place[2]
    for y in range(out.shape[0]):
        out[y, xl] = own_set[...]
        out[y, 1 - xl] = near_set[...]


def own_kernel(grads, pre, down, out):
    blocks, _, features = grads.shape
    hidden = sum(dot(grads[j], down[j * features:(j + 1) * features, :]) for j in range(blocks))
    out[...] = jnp.where(pre[...] > 0, hidden, 0.0).astype(out.dtype)


def terms_kernel(place, grads, own, pre_far, down_mine, down_other, up_own, up_mine, up_other, terms, up_far):
    core = place[0]
    blocks, features = grads.shape[0], grads.shape[2]
    half = blocks // 2
    units = up_mine.shape[0]
    up_far[pl.ds(pl.multiple_of(core * units, 16), units), :] = up_mine[...]
    up_far[pl.ds(pl.multiple_of((1 - core) * units, 16), units), :] = up_other[...]
    far = sum(
        dot(grads[core * half + j], down_mine[j * features:(j + 1) * features, :]) for j in range(half)
    ) + sum(
        dot(grads[(1 - core) * half + j], down_other[j * features:(j + 1) * features, :]) for j in range(half)
    )
    far = jnp.where(pre_far[...] > 0, far, 0.0).astype(jnp.bfloat16)
    terms[...] = (dot(own[...], up_own[...]) + dot(far, up_far[...])).astype(terms.dtype)


def down_kernel(place, grads, pre_own, pre_far, kept, sent):
    core, xh, xl, live = place[0], place[1], place[2], place[3]
    blocks, rows, features = grads.shape
    units = pre_own.shape[1]
    share = kept.shape[2]
    groups = features // (4 * share)
    at = lax.broadcasted_iota(jnp.int32, pre_own.shape, 0)
    part = rows // 4
    row = at + (at // part + xl) * part
    hidden = jnp.concatenate(
        [jnp.where(row < live, jnp.maximum(pre[...], 0), 0).astype(jnp.bfloat16) for pre in (pre_own, pre_far)],
        axis=1,
    )
    for j in range(blocks):
        block = lax.dot_general(
            grads[j], hidden, (((0,), (0,)), ((), ())), preferred_element_type=jnp.float32
        ).astype(kept.dtype)
        for g in range(groups):
            z = j * groups + g
            for h in range(2):
                first = (g * 4 + h * 2) * share
                low = block[first:first + share, :]
                high = block[first + share:first + 2 * share, :]
                mine = jnp.where(core == 0, low, high)
                other = jnp.where(core == 0, high, low)
                for t in range(2):
                    kind = t * 2 + jnp.abs(xh - h)
                    kept[kind, z] = mine[:, t * units:(t + 1) * units]
                    sent[kind, z] = other[:, t * units:(t + 1) * units]


def put(place, blocks, out, sems):
    y, xl = place[4], place[2]
    rows = blocks[0][0].shape[0] if len(blocks[0]) == 3 else blocks[0][4]
    ranks = out.shape[0] // (2 * rows)
    running = []
    for i, (block, dy, dx, *rest) in enumerate(blocks):
        at = ((y + dy + ranks) % ranks) * 2 + (1 - xl if dx else xl)
        start = pl.multiple_of(at * rows, 16)
        source = block.at[pl.ds(rest[0], rows)] if rest else block
        copy = pltpu.make_async_copy(source, out.at[pl.ds(start, rows)], sems.at[i])
        copy.start()
        running.append(copy)
    for copy in running:
        copy.wait()


def first_kernel(place, own, near, below, above, out, sems):
    put(place, [(own, 0, 0), (near, 0, 1), (below, -1, 0), (above, 1, 0)], out, sems)


def last_kernel(place, partial, across, beside, out, sems):
    rows = across.shape[0] // 2
    put(
        place,
        [(across, 2, 0, 0, rows), (across, 2, 1, rows, rows), (beside, -1, 1, 0, rows), (beside, 1, 1, rows, rows)],
        out,
        sems,
    )


def own_part(array, index, axis):
    return lax.dynamic_index_in_dim(array, index, axis, keepdims=False)


def on_device(grad_out, pre_act, up_weight, down_weight, slot_counts):
    slot_rows, features = grad_out.shape
    hidden_units = pre_act.shape[1]
    ys, zs = lax.axis_size("y"), lax.axis_size("z")
    reps = 2 * ys
    width = features * reps
    rows = slot_rows // reps
    half_rows = slot_rows // 2
    core, xh, xl, y = (lax.axis_index(a) for a in ("core", "xh", "xl", "y"))
    place = jnp.stack([core, xh, xl, slot_counts[0], y]).astype(jnp.int32)
    bf16 = jnp.bfloat16

    def turn(by):
        return [(i, (i + by) % ys) for i in range(ys)]

    params = pltpu.CompilerParams(vmem_limit_bytes=LIMIT)
    set_shape = jax.ShapeDtypeStruct((half_rows, features), bf16)
    pre_shape = jax.ShapeDtypeStruct((half_rows, hidden_units), bf16)
    own_set, other_set, pre_own, pre_sent = pl.pallas_call(
        split_kernel,
        out_shape=(set_shape, set_shape, pre_shape, pre_shape),
        in_specs=[SMEM] + [VMEM] * 2,
        out_specs=(VMEM,) * 4,
        compiler_params=params,
        name="split",
    )(place, grad_out, pre_act)
    near_set = lax.ppermute(other_set, "xl", NEAR)
    grads = pl.pallas_call(
        spread_kernel,
        out_shape=jax.ShapeDtypeStruct((ys, 2, half_rows, features), bf16),
        in_specs=[SMEM] + [VMEM] * 2,
        out_specs=VMEM,
        compiler_params=params,
        name="spread",
    )(place, own_set, near_set)
    grads = lax.all_to_all(grads, "y", 0, 0, tiled=True).reshape(reps, half_rows, features)
    pre_far = lax.ppermute(pre_sent, "xl", NEAR)

    down_mine = lax.ppermute(own_part(down_weight.reshape(2, width // 2, hidden_units), core, 0), RING, FAR)
    up_mine = lax.ppermute(
        own_part(up_weight.reshape(2, hidden_units // 2, width), core, 0), ("xh", "core", "xl"), MIXED
    )
    down_other = lax.ppermute(down_mine, "core", NEAR)
    up_other = lax.ppermute(up_mine, "core", NEAR)

    pre_grad = pl.pallas_call(
        own_kernel,
        out_shape=jax.ShapeDtypeStruct((half_rows, hidden_units), bf16),
        in_specs=[VMEM] * 3,
        out_specs=VMEM,
        compiler_params=pltpu.CompilerParams(vmem_limit_bytes=LIMIT),
        cost_estimate=pl.CostEstimate(
            flops=2 * half_rows * width * hidden_units, bytes_accessed=4 * width * hidden_units, transcendentals=0
        ),
        name="own_grad",
    )(grads, pre_own, down_weight)
    share = width // (4 * zs)
    laid_out = jax.ShapeDtypeStruct((4, zs, share, hidden_units), bf16)
    kept, sent = pl.pallas_call(
        down_kernel,
        out_shape=(laid_out, laid_out),
        in_specs=[SMEM] + [VMEM] * 3,
        out_specs=(VMEM, VMEM),
        compiler_params=pltpu.CompilerParams(vmem_limit_bytes=LIMIT),
        cost_estimate=pl.CostEstimate(
            flops=4 * half_rows * width * hidden_units, bytes_accessed=8 * width * hidden_units, transcendentals=0
        ),
        name="down_terms",
    )(place, grads, pre_own, pre_far)

    terms = pl.pallas_call(
        terms_kernel,
        out_shape=jax.ShapeDtypeStruct((half_rows, width), bf16),
        in_specs=[SMEM] + [VMEM] * 8,
        out_specs=VMEM,
        scratch_shapes=[pltpu.VMEM((hidden_units, width), bf16)],
        compiler_params=pltpu.CompilerParams(vmem_limit_bytes=LIMIT),
        cost_estimate=pl.CostEstimate(
            flops=6 * half_rows * width * hidden_units, bytes_accessed=12 * width * hidden_units, transcendentals=0
        ),
        name="terms",
    )(place, grads, pre_grad, pre_far, down_mine, down_other, up_weight, up_mine, up_other)

    f32 = jnp.float32
    came = lax.all_to_all(terms.reshape(ys, rows, width), "y", 0, 0, tiled=True)
    own = sum(came[i].astype(f32) for i in range(ys)).astype(bf16)

    other = lax.ppermute(sent, "core", NEAR)
    chip = [(kept[k].astype(f32) + other[k].astype(f32)) for k in range(4)]
    ring = [
        lax.ppermute(chip[2].astype(bf16), "xl", NEAR),
        lax.ppermute(chip[3].astype(bf16), RING, FAR),
        lax.ppermute(chip[1].astype(bf16), RING, ACROSS),
    ]

    near = lax.ppermute(own, "xl", NEAR)
    below = lax.ppermute(own, "y", turn(1))
    above = lax.ppermute(own, "y", turn(-1))

    own_chip, ring, _ = lax.optimization_barrier((chip[0].astype(bf16), ring, own))
    ring_sum = (own_chip.astype(f32) + sum(part.astype(f32) for part in ring)).astype(bf16)
    z_terms = lax.all_to_all(ring_sum, "z", 0, 0, tiled=True)
    down_grad = jnp.sum(z_terms.astype(f32), axis=0) / (4 * zs)

    near, below, above = lax.optimization_barrier((near, below, above))
    across = lax.ppermute(jnp.concatenate([own, near]), "y", turn(2))
    beside = lax.ppermute(jnp.concatenate([below, above]), "xl", NEAR)
    whole = jax.ShapeDtypeStruct((slot_rows, width), bf16)
    first = pl.pallas_call(
        first_kernel,
        out_shape=whole,
        in_specs=[SMEM] + [VMEM] * 4,
        out_specs=ANY,
        scratch_shapes=[pltpu.SemaphoreType.DMA((4,))],
        compiler_params=params,
        name="place_first",
    )(place, own, near, below, above)
    input_grad = pl.pallas_call(
        last_kernel,
        out_shape=whole,
        in_specs=[SMEM, ANY] + [VMEM] * 2,
        out_specs=ANY,
        scratch_shapes=[pltpu.SemaphoreType.DMA((4,))],
        input_output_aliases={1: 0},
        compiler_params=params,
        name="place_last",
    )(place, first, across, beside)
    return (input_grad, down_grad)


def solution(mesh):
    zs = mesh.shape["dp"] // 4
    ys = mesh.shape["rep"] // 2
    finer = Mesh(mesh.devices.reshape(zs, 2, 2, ys, 2), (*DP, *REP))
    in_specs = (P(DP, REP), P(DP, REP), P(REP, None), P(None, REP), P(DP))
    out_specs = (P(DP, None), P(DP, REP))
    return jax.shard_map(
        on_device, mesh=finer, in_specs=in_specs, out_specs=out_specs, check_vma=False
    )
```

```python
import jax
import jax.numpy as jnp
from jax import lax
from jax.experimental import pallas as pl
from jax.experimental.pallas import tpu as pltpu
from jax.sharding import Mesh
from jax.sharding import PartitionSpec as P

DP = ("zh", "zl", "xh", "core")
REP = ("y", "xl")
RING = ("xh", "xl")
NEAR = [(0, 1), (1, 0)]
FAR = [(0, 3), (3, 0), (1, 2), (2, 1)]
MIXED = [(i, i ^ 1 if i // 2 % 2 == 0 else i ^ 5) for i in range(8)]
ACROSS = [(0, 2), (2, 0), (1, 3), (3, 1)]
VMEM = pl.BlockSpec(memory_space=pltpu.VMEM)
SMEM = pl.BlockSpec(memory_space=pltpu.SMEM)
ANY = pl.BlockSpec(memory_space=pl.ANY)
LIMIT = 12 * 1024 * 1024


def dot(a, b):
    return jnp.dot(a, b, preferred_element_type=jnp.float32)


def split_kernel(place, whole, own, other):
    xl = place[2]
    part = own.shape[0] // 4
    for y in range(4):
        for x, out in ((xl, own), (1 - xl, other)):
            out[y * part:(y + 1) * part, :] = whole[pl.ds(pl.multiple_of((y * 2 + x) * part, 16), part), :]


def live_kernel(place, whole, own, other):
    xl, live = place[2], place[3]
    part = own.shape[0] // 4
    for y in range(4):
        for x, out in ((xl, own), (1 - xl, other)):
            first = pl.multiple_of((y * 2 + x) * part, 16)
            row = first + lax.broadcasted_iota(jnp.int32, (part, out.shape[1]), 0)
            out[y * part:(y + 1) * part, :] = jnp.where(row < live, whole[pl.ds(first, part), :], 0).astype(out.dtype)


def spread_kernel(place, own_set, near_set, out):
    xl = place[2]
    for y in range(out.shape[0]):
        out[y, xl] = own_set[...]
        out[y, 1 - xl] = near_set[...]


def own_kernel(grads, pre, down, out):
    blocks, _, features = grads.shape
    hidden = sum(dot(grads[j], down[j * features:(j + 1) * features, :]) for j in range(blocks))
    out[...] = jnp.where(pre[...] > 0, hidden, 0.0).astype(out.dtype)


def terms_kernel(place, grads, own, pre_far, down_mine, down_other, up_own, up_mine, up_other, terms, up_far):
    core = place[0]
    blocks, features = grads.shape[0], grads.shape[2]
    half = blocks // 2
    units = up_mine.shape[0]
    up_far[pl.ds(pl.multiple_of(core * units, 16), units), :] = up_mine[...]
    up_far[pl.ds(pl.multiple_of((1 - core) * units, 16), units), :] = up_other[...]
    far = sum(
        dot(grads[core * half + j], down_mine[j * features:(j + 1) * features, :]) for j in range(half)
    ) + sum(
        dot(grads[(1 - core) * half + j], down_other[j * features:(j + 1) * features, :]) for j in range(half)
    )
    far = jnp.where(pre_far[...] > 0, far, 0.0).astype(jnp.bfloat16)
    terms[...] = (dot(own[...], up_own[...]) + dot(far, up_far[...])).astype(terms.dtype)


def down_kernel(place, grads, pre_own, pre_far, kept, sent):
    core, xh, xl, live = place[0], place[1], place[2], place[3]
    blocks, rows, features = grads.shape
    units = pre_own.shape[1]
    share = kept.shape[2]
    groups = features // (4 * share)
    at = lax.broadcasted_iota(jnp.int32, pre_own.shape, 0)
    part = rows // 4
    row = at + (at // part + xl) * part
    hidden = jnp.concatenate(
        [jnp.where(row < live, jnp.maximum(pre[...], 0), 0).astype(jnp.bfloat16) for pre in (pre_own, pre_far)],
        axis=1,
    )
    for j in range(blocks):
        block = lax.dot_general(
            grads[j], hidden, (((0,), (0,)), ((), ())), preferred_element_type=jnp.float32
        ).astype(kept.dtype)
        for g in range(groups):
            zh, zl = divmod(j * groups + g, 4)
            z = zl * (kept.shape[1] // 4) + zh
            for h in range(2):
                first = (g * 4 + h * 2) * share
                low = block[first:first + share, :]
                high = block[first + share:first + 2 * share, :]
                mine = jnp.where(core == 0, low, high)
                other = jnp.where(core == 0, high, low)
                for t in range(2):
                    kind = t * 2 + jnp.abs(xh - h)
                    kept[kind, z] = mine[:, t * units:(t + 1) * units]
                    sent[kind, z] = other[:, t * units:(t + 1) * units]


def ring_kernel(own, near, far, across, out):
    total = own[...].astype(jnp.float32) + near[...].astype(jnp.float32)
    out[...] = (total + far[...].astype(jnp.float32) + across[...].astype(jnp.float32)).astype(out.dtype)


def put(place, blocks, out, sems):
    y, xl = place[4], place[2]
    rows = blocks[0][0].shape[0] if len(blocks[0]) == 3 else blocks[0][4]
    ranks = out.shape[0] // (2 * rows)
    running = []
    for i, (block, dy, dx, *rest) in enumerate(blocks):
        at = ((y + dy + ranks) % ranks) * 2 + (1 - xl if dx else xl)
        start = pl.multiple_of(at * rows, 16)
        source = block.at[pl.ds(rest[0], rows)] if rest else block
        copy = pltpu.make_async_copy(source, out.at[pl.ds(start, rows)], sems.at[i])
        copy.start()
        running.append(copy)
    for copy in running:
        copy.wait()


def first_kernel(place, own, near, below, above, out, sems):
    put(place, [(own, 0, 0), (near, 0, 1), (below, -1, 0), (above, 1, 0)], out, sems)


def last_kernel(place, partial, across, beside, out, sems):
    rows = across.shape[0] // 2
    put(
        place,
        [(across, 2, 0, 0, rows), (across, 2, 1, rows, rows), (beside, -1, 1, 0, rows), (beside, 1, 1, rows, rows)],
        out,
        sems,
    )


def own_part(array, index, axis):
    return lax.dynamic_index_in_dim(array, index, axis, keepdims=False)


def on_device(grad_out, pre_act, up_weight, down_weight, slot_counts):
    slot_rows, features = grad_out.shape
    hidden_units = pre_act.shape[1]
    ys, zs = lax.axis_size("y"), lax.axis_size(("zh", "zl"))
    reps = 2 * ys
    width = features * reps
    rows = slot_rows // reps
    half_rows = slot_rows // 2
    core, xh, xl, y = (lax.axis_index(a) for a in ("core", "xh", "xl", "y"))
    place = jnp.stack([core, xh, xl, slot_counts[0], y]).astype(jnp.int32)
    bf16 = jnp.bfloat16

    def turn(by):
        return [(i, (i + by) % ys) for i in range(ys)]

    params = pltpu.CompilerParams(vmem_limit_bytes=LIMIT)
    set_shape = jax.ShapeDtypeStruct((half_rows, features), bf16)
    pre_shape = jax.ShapeDtypeStruct((half_rows, hidden_units), bf16)
    own_set, other_set = pl.pallas_call(
        live_kernel,
        out_shape=(set_shape, set_shape),
        in_specs=[SMEM, VMEM],
        out_specs=(VMEM, VMEM),
        compiler_params=params,
        name="live_sets",
    )(place, grad_out)
    pre_own, pre_sent = pl.pallas_call(
        split_kernel,
        out_shape=(pre_shape, pre_shape),
        in_specs=[SMEM, VMEM],
        out_specs=(VMEM, VMEM),
        compiler_params=params,
        name="pre_sets",
    )(place, pre_act)
    near_set = lax.ppermute(other_set, "xl", NEAR)
    grads = pl.pallas_call(
        spread_kernel,
        out_shape=jax.ShapeDtypeStruct((ys, 2, half_rows, features), bf16),
        in_specs=[SMEM] + [VMEM] * 2,
        out_specs=VMEM,
        compiler_params=params,
        name="spread",
    )(place, own_set, near_set)
    grads = lax.all_to_all(grads, "y", 0, 0, tiled=True).reshape(reps, half_rows, features)
    pre_far = lax.ppermute(pre_sent, "xl", NEAR)

    down_mine = lax.ppermute(own_part(down_weight.reshape(2, width // 2, hidden_units), core, 0), RING, FAR)
    up_mine = lax.ppermute(
        own_part(up_weight.reshape(2, hidden_units // 2, width), core, 0), ("xh", "core", "xl"), MIXED
    )
    down_other = lax.ppermute(down_mine, "core", NEAR)
    up_other = lax.ppermute(up_mine, "core", NEAR)

    pre_grad = pl.pallas_call(
        own_kernel,
        out_shape=jax.ShapeDtypeStruct((half_rows, hidden_units), bf16),
        in_specs=[VMEM] * 3,
        out_specs=VMEM,
        compiler_params=pltpu.CompilerParams(vmem_limit_bytes=LIMIT),
        cost_estimate=pl.CostEstimate(
            flops=2 * half_rows * width * hidden_units, bytes_accessed=4 * width * hidden_units, transcendentals=0
        ),
        name="own_grad",
    )(grads, pre_own, down_weight)
    share = width // (4 * zs)
    laid_out = jax.ShapeDtypeStruct((4, zs, share, hidden_units), bf16)
    kept, sent = pl.pallas_call(
        down_kernel,
        out_shape=(laid_out, laid_out),
        in_specs=[SMEM] + [VMEM] * 3,
        out_specs=(VMEM, VMEM),
        compiler_params=pltpu.CompilerParams(vmem_limit_bytes=LIMIT),
        cost_estimate=pl.CostEstimate(
            flops=4 * half_rows * width * hidden_units, bytes_accessed=8 * width * hidden_units, transcendentals=0
        ),
        name="down_terms",
    )(place, grads, pre_own, pre_far)

    share = width // (4 * zs)
    laid_out = jax.ShapeDtypeStruct((4, zs, share, hidden_units), bf16)
    kept, sent = pl.pallas_call(
        down_kernel,
        out_shape=(laid_out, laid_out),
        in_specs=[SMEM] + [VMEM] * 3,
        out_specs=(VMEM, VMEM),
        compiler_params=pltpu.CompilerParams(vmem_limit_bytes=LIMIT),
        cost_estimate=pl.CostEstimate(
            flops=4 * half_rows * width * hidden_units, bytes_accessed=8 * width * hidden_units, transcendentals=0
        ),
        name="down_terms",
    )(place, grads, pre_own, pre_far)

    pre_later, sent = lax.optimization_barrier((pre_far, sent))
    terms = pl.pallas_call(
        terms_kernel,
        out_shape=jax.ShapeDtypeStruct((half_rows, width), bf16),
        in_specs=[SMEM] + [VMEM] * 8,
        out_specs=VMEM,
        scratch_shapes=[pltpu.VMEM((hidden_units, width), bf16)],
        compiler_params=pltpu.CompilerParams(vmem_limit_bytes=LIMIT),
        cost_estimate=pl.CostEstimate(
            flops=6 * half_rows * width * hidden_units, bytes_accessed=12 * width * hidden_units, transcendentals=0
        ),
        name="terms",
    )(place, grads, pre_grad, pre_later, down_mine, down_other, up_weight, up_mine, up_other)

    f32 = jnp.float32
    came = lax.all_to_all(terms.reshape(ys, rows, width), "y", 0, 0, tiled=True)
    own = sum(came[i].astype(f32) for i in range(ys)).astype(bf16)

    other = lax.ppermute(sent, "core", NEAR)
    chip = [(kept[k].astype(f32) + other[k].astype(f32)) for k in range(4)]
    ring = [
        lax.ppermute(chip[2].astype(bf16), "xl", NEAR),
        lax.ppermute(chip[3].astype(bf16), RING, FAR),
        lax.ppermute(chip[1].astype(bf16), RING, ACROSS),
    ]

    near = lax.ppermute(own, "xl", NEAR)
    below = lax.ppermute(own, "y", turn(1))
    above = lax.ppermute(own, "y", turn(-1))

    own_chip, ring, _ = lax.optimization_barrier((chip[0].astype(bf16), ring, own))
    ring_sum = pl.pallas_call(
        ring_kernel,
        out_shape=jax.ShapeDtypeStruct((zs, share, hidden_units), bf16),
        in_specs=[VMEM] * 4,
        out_specs=VMEM,
        compiler_params=params,
        cost_estimate=pl.CostEstimate(flops=2 * width * hidden_units, bytes_accessed=10 * width * hidden_units, transcendentals=0),
        name="ring_sum",
    )(own_chip, *ring)
    low_terms = lax.all_to_all(ring_sum, "zl", 0, 0, tiled=True).reshape(4, zs // 4, share, hidden_units)
    low_sum = sum(low_terms[i].astype(f32) for i in range(4))
    highs = zs // 4
    high = lax.axis_index("zh")
    high_sum = own_part(low_sum, high, 0)
    for step in range(1, highs):
        part = own_part(low_sum, lax.rem(high + step, highs), 0)
        high_sum += lax.ppermute(part, "zh", [(i, (i + step) % highs) for i in range(highs)])
    down_grad = high_sum / (4 * zs)

    near, below, above = lax.optimization_barrier((near, below, above))
    across = lax.ppermute(jnp.concatenate([own, near]), "y", turn(2))
    beside = lax.ppermute(jnp.concatenate([below, above]), "xl", NEAR)
    whole = jax.ShapeDtypeStruct((slot_rows, width), bf16)
    first = pl.pallas_call(
        first_kernel,
        out_shape=whole,
        in_specs=[SMEM] + [VMEM] * 4,
        out_specs=ANY,
        scratch_shapes=[pltpu.SemaphoreType.DMA((4,))],
        compiler_params=params,
        name="place_first",
    )(place, own, near, below, above)
    input_grad = pl.pallas_call(
        last_kernel,
        out_shape=whole,
        in_specs=[SMEM, ANY] + [VMEM] * 2,
        out_specs=ANY,
        scratch_shapes=[pltpu.SemaphoreType.DMA((4,))],
        input_output_aliases={1: 0},
        compiler_params=params,
        name="place_last",
    )(place, first, across, beside)
    return (input_grad, down_grad)


def solution(mesh):
    zs = mesh.shape["dp"] // 4
    ys = mesh.shape["rep"] // 2
    finer = Mesh(mesh.devices.reshape(zs // 4, 4, 2, 2, ys, 2), (*DP, *REP))
    in_specs = (P(DP, REP), P(DP, REP), P(REP, None), P(None, REP), P(DP))
    out_specs = (P(DP, None), P(DP, REP))
    return jax.shard_map(
        on_device, mesh=finer, in_specs=in_specs, out_specs=out_specs, check_vma=False
    )
```

```python
import jax
import jax.numpy as jnp
from jax import lax
from jax.experimental import pallas as pl
from jax.experimental.pallas import tpu as pltpu
from jax.sharding import Mesh
from jax.sharding import PartitionSpec as P

DP = ("zh", "zl", "xh", "core")
REP = ("y", "xl")
RING = ("xh", "xl")
NEAR = [(0, 1), (1, 0)]
FAR = [(0, 3), (3, 0), (1, 2), (2, 1)]
MIXED = [(i, i ^ 1 if i // 2 % 2 == 0 else i ^ 5) for i in range(8)]
ACROSS = [(0, 2), (2, 0), (1, 3), (3, 1)]
VMEM = pl.BlockSpec(memory_space=pltpu.VMEM)
SMEM = pl.BlockSpec(memory_space=pltpu.SMEM)
ANY = pl.BlockSpec(memory_space=pl.ANY)
FIRST = 400
LIMIT = 12 * 1024 * 1024


def dot(a, b):
    return jnp.dot(a, b, preferred_element_type=jnp.float32)


def own_rows(ref, xl):
    part = ref.shape[0] // 8
    return jnp.concatenate(
        [ref[pl.ds(pl.multiple_of((y * 2 + xl) * part, 16), part), :] for y in range(4)], axis=0
    )


def sent_kernel(place, whole, other):
    other[...] = own_rows(whole, 1 - place[2])


def live_kernel(place, whole, own, other):
    xl, live = place[2], place[3]
    ranks = own.shape[0]
    part = other.shape[0] // 4
    for y in range(4):
        for x in (0, 1):
            first = pl.multiple_of((y * 2 + (1 - xl if x else xl)) * part, 16)
            row = first + lax.broadcasted_iota(jnp.int32, (part, other.shape[1]), 0)
            rows = jnp.where(row < live, whole[pl.ds(first, part), :], 0).astype(other.dtype)
            if x:
                other[y * part:(y + 1) * part, :] = rows
            else:
                for rank in range(ranks):
                    own[rank, y * part:(y + 1) * part, :] = rows


def spread_kernel(block, out):
    for rank in range(out.shape[0]):
        out[rank] = block[...]


def own_kernel(place, grads, grads_near, pre, down, out):
    xl = place[2]
    blocks, _, features = grads.shape
    hidden = sum(
        dot(g[j], down[pl.ds(pl.multiple_of((2 * j + x) * features, 16), features), :])
        for g, x in ((grads, xl), (grads_near, 1 - xl))
        for j in range(blocks)
    )
    out[...] = jnp.where(own_rows(pre, xl) > 0, hidden, 0.0).astype(out.dtype)


def terms_kernel(
    place, grads, grads_near, own, pre_far, down_mine, down_other, up_own, up_mine, up_other, terms, up_far
):
    core, xl = place[0], place[2]
    blocks, features = grads.shape[0], grads.shape[2]
    half = blocks // 2
    units = up_mine.shape[0]
    up_far[pl.ds(pl.multiple_of(core * units, 16), units), :] = up_mine[...]
    up_far[pl.ds(pl.multiple_of((1 - core) * units, 16), units), :] = up_other[...]
    far = sum(
        dot(g[c * half + j], down[pl.ds(pl.multiple_of((2 * j + x) * features, 16), features), :])
        for g, x in ((grads, xl), (grads_near, 1 - xl))
        for c, down in ((core, down_mine), (1 - core, down_other))
        for j in range(half)
    )
    far = jnp.where(pre_far[...] > 0, far, 0.0).astype(jnp.bfloat16)
    columns = terms.shape[1] // 4
    for i in range(4):
        at = slice(i * columns, (i + 1) * columns)
        terms[:, at] = (dot(own[...], up_own[:, at]) + dot(far, up_far[:, at])).astype(terms.dtype)


def down_kernel(place, grads, pre_own, pre_far, kept, sent):
    core, xh, xl, live = place[0], place[1], place[2], place[3]
    blocks, rows, features = grads.shape
    units = pre_far.shape[1]
    share = kept.shape[3]
    groups = features // (4 * share)
    at = lax.broadcasted_iota(jnp.int32, pre_far.shape, 0)
    part = rows // 4
    row = at + (at // part + xl) * part
    hidden = jnp.concatenate(
        [
            jnp.where(row < live, jnp.maximum(pre, 0), 0).astype(jnp.bfloat16)
            for pre in (own_rows(pre_own, xl), pre_far[...])
        ],
        axis=1,
    )
    for j in range(blocks):
        block = lax.dot_general(
            grads[j], hidden, (((0,), (0,)), ((), ())), preferred_element_type=jnp.float32
        ).astype(kept.dtype)
        for g in range(groups):
            for h in range(2):
                first = (g * 4 + h * 2) * share
                low = block[first:first + share, :]
                high = block[first + share:first + 2 * share, :]
                mine = jnp.where(core == 0, low, high)
                other = jnp.where(core == 0, high, low)
                for t in range(2):
                    kind = t * 2 + jnp.abs(xh - h)
                    kept[kind, g, j] = mine[:, t * units:(t + 1) * units]
                    sent[kind, g, j] = other[:, t * units:(t + 1) * units]


def chip_kernel(place, kept, came, kept_near, came_near, *outs):
    xl = place[2]
    groups = kept.shape[1]
    for kind, out in enumerate(outs):
        for ours, theirs, x in ((kept, came, xl), (kept_near, came_near, 1 - xl)):
            for g in range(groups):
                total = ours[kind, g].astype(jnp.float32) + theirs[kind, g].astype(jnp.float32)
                out[x * groups + g] = total.astype(out.dtype)


def ring_kernel(own, near, far, across, out):
    total = own[...].astype(jnp.float32) + near[...].astype(jnp.float32)
    out[...] = (total + far[...].astype(jnp.float32) + across[...].astype(jnp.float32)).astype(out.dtype)


def rows_kernel(came, out):
    out[...] = sum(came[i].astype(jnp.float32) for i in range(came.shape[0])).astype(out.dtype)


def put(place, blocks, out, sems):
    y, xl = place[4], place[2]
    rows = blocks[0][0].shape[0] if len(blocks[0]) == 3 else blocks[0][4]
    ranks = out.shape[0] // (2 * rows)
    running = []
    for i, (block, dy, dx, *rest) in enumerate(blocks):
        at = ((y + dy + ranks) % ranks) * 2 + (1 - xl if dx else xl)
        start = pl.multiple_of(at * rows, 16)
        source = block.at[pl.ds(rest[0], rows)] if rest else block
        copy = pltpu.make_async_copy(source, out.at[pl.ds(start, rows)], sems.at[i])
        copy.start()
        running.append(copy)
    for copy in running:
        copy.wait()


def first_kernel(place, own, near, below, above, out, sems):
    put(place, [(own, 0, 0), (near, 0, 1), (below, -1, 0), (above, 1, 0)], out, sems)


def last_kernel(place, partial, across, beside, out, sems):
    rows = across.shape[0] // 2
    put(
        place,
        [(across, 2, 0, 0, rows), (across, 2, 1, rows, rows), (beside, -1, 1, 0, rows), (beside, 1, 1, rows, rows)],
        out,
        sems,
    )


def own_part(array, index, axis):
    return lax.dynamic_index_in_dim(array, index, axis, keepdims=False)


def on_device(grad_out, pre_act, up_weight, down_weight, slot_counts):
    slot_rows, features = grad_out.shape
    hidden_units = pre_act.shape[1]
    ys, zs = lax.axis_size("y"), lax.axis_size(("zh", "zl"))
    reps = 2 * ys
    width = features * reps
    rows = slot_rows // reps
    half_rows = slot_rows // 2
    core, xh, xl, y = (lax.axis_index(a) for a in ("core", "xh", "xl", "y"))
    place = jnp.stack([core, xh, xl, slot_counts[0], y]).astype(jnp.int32)
    bf16 = jnp.bfloat16

    def turn(by):
        return [(i, (i + by) % ys) for i in range(ys)]

    f32 = jnp.float32

    def call(kernel, name, outs, *operands, flops=0, scratch=()):
        size = sum(x.size * x.dtype.itemsize for x in operands)
        return pl.pallas_call(
            kernel,
            out_shape=outs,
            in_specs=[SMEM if x is place else VMEM for x in operands],
            out_specs=tuple(VMEM for _ in outs) if isinstance(outs, tuple) else VMEM,
            scratch_shapes=list(scratch),
            compiler_params=pltpu.CompilerParams(vmem_limit_bytes=LIMIT),
            cost_estimate=pl.CostEstimate(flops=flops, bytes_accessed=size, transcendentals=0),
            name=name,
        )(*operands)

    def like(*shape):
        return jax.ShapeDtypeStruct(shape, bf16)

    own_sets, other_set = call(
        live_kernel, "live_sets", (like(ys, half_rows, features), like(half_rows, features)), place, grad_out
    )
    grads = lax.all_to_all(own_sets, "y", 0, 0, tiled=True)
    pre_sent = call(sent_kernel, "pre_sent", like(half_rows, hidden_units), place, pre_act)
    pre_far = lax.ppermute(pre_sent, "xl", NEAR)
    down_tied, other_set = lax.optimization_barrier((down_weight, other_set))
    near_set = lax.ppermute(other_set, "xl", NEAR)
    up_tied, near_set = lax.optimization_barrier((up_weight, near_set))
    near_sets = call(spread_kernel, "spread", like(ys, half_rows, features), near_set)
    grads, near_sets, pre_far = lax.optimization_barrier((grads, near_sets, pre_far))
    grads_near = lax.all_to_all(near_sets, "y", 0, 0, tiled=True)
    down_mine = lax.ppermute(own_part(down_tied.reshape(2, width // 2, hidden_units), core, 0), RING, FAR)
    up_mine = lax.ppermute(
        own_part(up_tied.reshape(2, hidden_units // 2, width), core, 0), ("xh", "core", "xl"), MIXED
    )

    share = width // (4 * zs)
    laid_out = like(4, 2, zs // 4, share, hidden_units)
    flops = half_rows * width * hidden_units
    kept, sent = call(down_kernel, "down_own", (laid_out, laid_out), place, grads, pre_act, pre_far, flops=FIRST * flops)
    down_mine, up_mine, grads_near, sent = lax.optimization_barrier((down_mine, up_mine, grads_near, sent))
    down_other = lax.ppermute(down_mine, "core", NEAR)
    up_other = lax.ppermute(up_mine, "core", NEAR)
    came = lax.ppermute(sent, "core", NEAR)
    kept_near, sent_near = call(
        down_kernel, "down_near", (laid_out, laid_out), place, grads_near, pre_act, pre_far, flops=2 * flops
    )
    came_near = lax.ppermute(sent_near, "core", NEAR)

    pre_grad = call(
        own_kernel, "own_grad", like(half_rows, hidden_units), place, grads, grads_near, pre_act, down_weight,
        flops=2 * flops,
    )
    pre_later, sent_near = lax.optimization_barrier((pre_far, sent_near))
    terms = call(
        terms_kernel, "terms", like(half_rows, width),
        place, grads, grads_near, pre_grad, pre_later, down_mine, down_other, up_weight, up_mine, up_other,
        flops=6 * flops, scratch=[pltpu.VMEM((hidden_units, width), bf16)],
    )
    terms = lax.all_to_all(terms.reshape(ys, rows, width), "y", 0, 0, tiled=True)
    own = call(rows_kernel, "own_rows", like(rows, width), terms)

    kind = like(4, zs // 4, share, hidden_units)
    own_chip, across_chip, near_chip, far_chip = call(
        chip_kernel, "chip_sum", (kind,) * 4, place, kept, came, kept_near, came_near
    )
    ring = [
        lax.ppermute(near_chip, "xl", NEAR),
        lax.ppermute(far_chip, RING, FAR),
        lax.ppermute(across_chip, RING, ACROSS),
    ]

    near = lax.ppermute(own, "xl", NEAR)
    below = lax.ppermute(own, "y", turn(1))
    above = lax.ppermute(own, "y", turn(-1))

    own_chip, ring, _ = lax.optimization_barrier((own_chip, ring, own))
    ring_sum = call(ring_kernel, "ring_sum", kind, own_chip, *ring)
    low_terms = lax.all_to_all(ring_sum, "zl", 0, 0, tiled=True)
    low_sum = call(rows_kernel, "low_sum", like(zs // 4, share, hidden_units), low_terms)
    high_terms = lax.all_to_all(low_sum, "zh", 0, 0, tiled=True)
    down_grad = sum(high_terms[i].astype(f32) for i in range(zs // 4)) / (4 * zs)

    near, below, above = lax.optimization_barrier((near, below, above))
    across = lax.ppermute(jnp.concatenate([own, near]), "y", turn(2))
    beside = lax.ppermute(jnp.concatenate([below, above]), "xl", NEAR)
    whole = jax.ShapeDtypeStruct((slot_rows, width), bf16)
    first = pl.pallas_call(
        first_kernel,
        out_shape=whole,
        in_specs=[SMEM] + [VMEM] * 4,
        out_specs=ANY,
        scratch_shapes=[pltpu.SemaphoreType.DMA((4,))],
        compiler_params=pltpu.CompilerParams(vmem_limit_bytes=LIMIT),
        name="place_first",
    )(place, own, near, below, above)
    input_grad = pl.pallas_call(
        last_kernel,
        out_shape=whole,
        in_specs=[SMEM, ANY] + [VMEM] * 2,
        out_specs=ANY,
        scratch_shapes=[pltpu.SemaphoreType.DMA((4,))],
        input_output_aliases={1: 0},
        compiler_params=pltpu.CompilerParams(vmem_limit_bytes=LIMIT),
        name="place_last",
    )(place, first, across, beside)
    return (input_grad, down_grad)


def solution(mesh):
    zs = mesh.shape["dp"] // 4
    ys = mesh.shape["rep"] // 2
    finer = Mesh(mesh.devices.reshape(zs // 4, 4, 2, 2, ys, 2), (*DP, *REP))
    in_specs = (P(DP, REP), P(DP, REP), P(REP, None), P(None, REP), P(DP))
    out_specs = (P(DP, None), P(DP, REP))
    return jax.shard_map(
        on_device, mesh=finer, in_specs=in_specs, out_specs=out_specs, check_vma=False
    )
```

```python
import jax
import jax.numpy as jnp
from jax import lax
from jax.experimental import pallas as pl
from jax.experimental.pallas import tpu as pltpu
from jax.sharding import Mesh
from jax.sharding import PartitionSpec as P

DP = ("z", "xh", "core")
REP = ("y", "xl")
RING = ("xh", "xl")
NEAR = [(0, 1), (1, 0)]
FAR = [(0, 3), (3, 0), (1, 2), (2, 1)]
MIXED = [(i, i ^ 1 if i // 2 % 2 == 0 else i ^ 5) for i in range(8)]
ACROSS = [(0, 2), (2, 0), (1, 3), (3, 1)]
VMEM = pl.BlockSpec(memory_space=pltpu.VMEM)
SMEM = pl.BlockSpec(memory_space=pltpu.SMEM)
ANY = pl.BlockSpec(memory_space=pl.ANY)
HBM = pl.BlockSpec(memory_space=pltpu.HBM)
LIMIT = 12 * 1024 * 1024


def dot(a, b):
    return jnp.dot(a, b, preferred_element_type=jnp.float32)


def own_rows(ref, xl):
    part = ref.shape[0] // 8
    return jnp.concatenate(
        [ref[pl.ds(pl.multiple_of((y * 2 + xl) * part, 16), part), :] for y in range(4)], axis=0
    )


def sent_kernel(place, whole, other):
    other[...] = own_rows(whole, 1 - place[2])


def live_kernel(place, whole, own, other):
    xl, live = place[2], place[3]
    part = own.shape[0] // 4
    for y in range(4):
        for x, out in ((xl, own), (1 - xl, other)):
            first = pl.multiple_of((y * 2 + x) * part, 16)
            row = first + lax.broadcasted_iota(jnp.int32, (part, out.shape[1]), 0)
            out[y * part:(y + 1) * part, :] = jnp.where(row < live, whole[pl.ds(first, part), :], 0).astype(out.dtype)


def spread_kernel(place, own_set, near_set, out):
    xl = place[2]
    for y in range(out.shape[0]):
        out[y, xl] = own_set[...]
        out[y, 1 - xl] = near_set[...]


def own_kernel(place, grads, pre, down, out):
    blocks, _, features = grads.shape
    hidden = sum(dot(grads[j], down[j * features:(j + 1) * features, :]) for j in range(blocks))
    out[...] = jnp.where(own_rows(pre, place[2]) > 0, hidden, 0.0).astype(out.dtype)


def terms_kernel(place, grads, own, pre_far, down_mine, down_other, up_own, up_mine, up_other, out, up_far, terms, sems):
    core = place[0]
    blocks, features = grads.shape[0], grads.shape[2]
    half = blocks // 2
    units = up_mine.shape[0]
    up_far[pl.ds(pl.multiple_of(core * units, 16), units), :] = up_mine[...]
    up_far[pl.ds(pl.multiple_of((1 - core) * units, 16), units), :] = up_other[...]
    far = sum(
        dot(grads[core * half + j], down_mine[j * features:(j + 1) * features, :]) for j in range(half)
    ) + sum(
        dot(grads[(1 - core) * half + j], down_other[j * features:(j + 1) * features, :]) for j in range(half)
    )
    far = jnp.where(pre_far[...] > 0, far, 0.0).astype(jnp.bfloat16)
    parts = sems.shape[0]
    columns = terms.shape[1] // parts
    running = []
    for i in range(parts):
        at = pl.ds(i * columns, columns)
        terms[:, at] = (dot(own[...], up_own[:, at]) + dot(far, up_far[:, at])).astype(terms.dtype)
        copy = pltpu.make_async_copy(terms.at[:, at], out.at[:, at], sems.at[i])
        copy.start()
        running.append(copy)
    for copy in running:
        copy.wait()


def down_kernel(place, grads, pre_own, pre_far, kept_out, sent_out, kept, sent, sems):
    core, xh, xl, live = place[0], place[1], place[2], place[3]
    blocks, rows, features = grads.shape
    units = pre_far.shape[1]
    share = kept.shape[2]
    groups = features // (4 * share)
    at = lax.broadcasted_iota(jnp.int32, pre_far.shape, 0)
    part = rows // 4
    row = at + (at // part + xl) * part
    hidden = jnp.concatenate(
        [jnp.where(row < live, jnp.maximum(pre, 0), 0).astype(jnp.bfloat16) for pre in (own_rows(pre_own, xl), pre_far[...])],
        axis=1,
    )
    running = []
    for j in range(blocks):
        block = lax.dot_general(
            grads[j], hidden, (((0,), (0,)), ((), ())), preferred_element_type=jnp.float32
        ).astype(kept.dtype)
        for g in range(groups):
            z = j * groups + g
            for h in range(2):
                first = (g * 4 + h * 2) * share
                low = block[first:first + share, :]
                high = block[first + share:first + 2 * share, :]
                mine = jnp.where(core == 0, low, high)
                other = jnp.where(core == 0, high, low)
                for t in range(2):
                    kind = t * 2 + jnp.abs(xh - h)
                    kept[kind, z] = mine[:, t * units:(t + 1) * units]
                    sent[kind, z] = other[:, t * units:(t + 1) * units]
        at = pl.ds(j * groups, groups)
        for i, (source, out) in enumerate(((sent, sent_out), (kept, kept_out))):
            copy = pltpu.make_async_copy(source.at[:, at], out.at[:, at], sems.at[i, j])
            copy.start()
            running.append(copy)
    for copy in running:
        copy.wait()


def ring_kernel(own, near, far, across, out):
    total = own[...].astype(jnp.float32) + near[...].astype(jnp.float32)
    out[...] = (total + far[...].astype(jnp.float32) + across[...].astype(jnp.float32)).astype(out.dtype)


def rows_kernel(came, out):
    out[...] = sum(came[i].astype(jnp.float32) for i in range(came.shape[0])).astype(out.dtype)


def chip_kernel(kept, came, *outs):
    for kind, out in enumerate(outs):
        out[...] = (kept[kind].astype(jnp.float32) + came[kind].astype(jnp.float32)).astype(out.dtype)


def put(place, blocks, out, sems):
    y, xl = place[4], place[2]
    rows = blocks[0][0].shape[0] if len(blocks[0]) == 3 else blocks[0][4]
    ranks = out.shape[0] // (2 * rows)
    running = []
    for i, (block, dy, dx, *rest) in enumerate(blocks):
        at = ((y + dy + ranks) % ranks) * 2 + (1 - xl if dx else xl)
        start = pl.multiple_of(at * rows, 16)
        source = block.at[pl.ds(rest[0], rows)] if rest else block
        copy = pltpu.make_async_copy(source, out.at[pl.ds(start, rows)], sems.at[i])
        copy.start()
        running.append(copy)
    for copy in running:
        copy.wait()


def first_kernel(place, own, near, below, above, out, sems):
    put(place, [(own, 0, 0), (near, 0, 1), (below, -1, 0), (above, 1, 0)], out, sems)


def last_kernel(place, partial, across, beside, out, sems):
    rows = across.shape[0] // 2
    put(
        place,
        [(across, 2, 0, 0, rows), (across, 2, 1, rows, rows), (beside, -1, 1, 0, rows), (beside, 1, 1, rows, rows)],
        out,
        sems,
    )


def own_part(array, index, axis):
    return lax.dynamic_index_in_dim(array, index, axis, keepdims=False)


def on_device(grad_out, pre_act, up_weight, down_weight, slot_counts):
    slot_rows, features = grad_out.shape
    hidden_units = pre_act.shape[1]
    ys, zs = lax.axis_size("y"), lax.axis_size("z")
    reps = 2 * ys
    width = features * reps
    rows = slot_rows // reps
    half_rows = slot_rows // 2
    core, xh, xl, y = (lax.axis_index(a) for a in ("core", "xh", "xl", "y"))
    place = jnp.stack([core, xh, xl, slot_counts[0], y]).astype(jnp.int32)
    bf16 = jnp.bfloat16

    def turn(by):
        return [(i, (i + by) % ys) for i in range(ys)]

    params = pltpu.CompilerParams(vmem_limit_bytes=LIMIT)
    set_shape = jax.ShapeDtypeStruct((half_rows, features), bf16)
    pre_shape = jax.ShapeDtypeStruct((half_rows, hidden_units), bf16)
    own_set, other_set = pl.pallas_call(
        live_kernel,
        out_shape=(set_shape, set_shape),
        in_specs=[SMEM, VMEM],
        out_specs=(VMEM, VMEM),
        compiler_params=params,
        name="live_sets",
    )(place, grad_out)
    pre_sent = pl.pallas_call(
        sent_kernel,
        out_shape=pre_shape,
        in_specs=[SMEM, VMEM],
        out_specs=VMEM,
        compiler_params=params,
        name="pre_sent",
    )(place, pre_act)
    near_set = lax.ppermute(other_set, "xl", NEAR)
    down_sent = own_part(down_weight.reshape(2, width // 2, hidden_units), core, 0)
    near_set, _ = lax.optimization_barrier((near_set, down_sent))
    grads = pl.pallas_call(
        spread_kernel,
        out_shape=jax.ShapeDtypeStruct((ys, 2, half_rows, features), bf16),
        in_specs=[SMEM] + [VMEM] * 2,
        out_specs=VMEM,
        compiler_params=params,
        name="spread",
    )(place, own_set, near_set)
    grads = lax.all_to_all(grads, "y", 0, 0, tiled=True).reshape(reps, half_rows, features)
    pre_far = lax.ppermute(pre_sent, "xl", NEAR)

    down_mine = lax.ppermute(down_sent, RING, FAR)
    up_mine = lax.ppermute(
        own_part(up_weight.reshape(2, hidden_units // 2, width), core, 0), ("xh", "core", "xl"), MIXED
    )
    down_other = lax.ppermute(down_mine, "core", NEAR)
    up_other = lax.ppermute(up_mine, "core", NEAR)

    pre_grad = pl.pallas_call(
        own_kernel,
        out_shape=jax.ShapeDtypeStruct((half_rows, hidden_units), bf16),
        in_specs=[SMEM] + [VMEM] * 3,
        out_specs=VMEM,
        compiler_params=pltpu.CompilerParams(vmem_limit_bytes=LIMIT),
        cost_estimate=pl.CostEstimate(
            flops=2 * half_rows * width * hidden_units, bytes_accessed=4 * width * hidden_units, transcendentals=0
        ),
        name="own_grad",
    )(place, grads, pre_act, down_weight)
    share = width // (4 * zs)
    laid_out = jax.ShapeDtypeStruct((4, zs, share, hidden_units), bf16)
    kept, sent = pl.pallas_call(
        down_kernel,
        out_shape=(laid_out, laid_out),
        in_specs=[SMEM] + [VMEM] * 3,
        out_specs=(HBM, HBM),
        scratch_shapes=[pltpu.VMEM(laid_out.shape, bf16)] * 2 + [pltpu.SemaphoreType.DMA((2, reps))],
        compiler_params=pltpu.CompilerParams(vmem_limit_bytes=LIMIT),
        cost_estimate=pl.CostEstimate(
            flops=4 * half_rows * width * hidden_units, bytes_accessed=8 * width * hidden_units, transcendentals=0
        ),
        name="down_terms",
    )(place, grads, pre_act, pre_far)

    pre_later, sent = lax.optimization_barrier((pre_far, sent))
    terms = pl.pallas_call(
        terms_kernel,
        out_shape=jax.ShapeDtypeStruct((half_rows, width), bf16),
        in_specs=[SMEM] + [VMEM] * 8,
        out_specs=HBM,
        scratch_shapes=[
            pltpu.VMEM((hidden_units, width), bf16),
            pltpu.VMEM((half_rows, width), bf16),
            pltpu.SemaphoreType.DMA((4,)),
        ],
        compiler_params=pltpu.CompilerParams(vmem_limit_bytes=LIMIT),
        cost_estimate=pl.CostEstimate(
            flops=6 * half_rows * width * hidden_units, bytes_accessed=12 * width * hidden_units, transcendentals=0
        ),
        name="terms",
    )(place, grads, pre_grad, pre_later, down_mine, down_other, up_weight, up_mine, up_other)

    f32 = jnp.float32
    came = lax.all_to_all(terms.reshape(ys, rows, width), "y", 0, 0, tiled=True)
    own = pl.pallas_call(
        rows_kernel,
        out_shape=jax.ShapeDtypeStruct((rows, width), bf16),
        in_specs=[VMEM],
        out_specs=VMEM,
        compiler_params=params,
        name="own_rows",
    )(came)

    other = lax.ppermute(sent, "core", NEAR)
    kind = jax.ShapeDtypeStruct((zs, share, hidden_units), bf16)
    own_chip, across_chip, near_chip, far_chip = pl.pallas_call(
        chip_kernel,
        out_shape=(kind,) * 4,
        in_specs=[VMEM] * 2,
        out_specs=(VMEM,) * 4,
        compiler_params=params,
        name="chip_sum",
    )(kept, other)
    ring = [
        lax.ppermute(near_chip, "xl", NEAR),
        lax.ppermute(far_chip, RING, FAR),
        lax.ppermute(across_chip, RING, ACROSS),
    ]

    near = lax.ppermute(own, "xl", NEAR)
    below = lax.ppermute(own, "y", turn(1))
    above = lax.ppermute(own, "y", turn(-1))

    own_chip, ring, _ = lax.optimization_barrier((own_chip, ring, own))
    ring_sum = pl.pallas_call(
        ring_kernel,
        out_shape=jax.ShapeDtypeStruct((zs, share, hidden_units), bf16),
        in_specs=[VMEM] * 4,
        out_specs=VMEM,
        compiler_params=params,
        cost_estimate=pl.CostEstimate(flops=2 * width * hidden_units, bytes_accessed=10 * width * hidden_units, transcendentals=0),
        name="ring_sum",
    )(own_chip, *ring)
    z_terms = lax.all_to_all(ring_sum, "z", 0, 0, tiled=True)
    down_grad = jnp.sum(z_terms.astype(f32), axis=0) / (4 * zs)

    near, below, above = lax.optimization_barrier((near, below, above))
    across = lax.ppermute(jnp.concatenate([own, near]), "y", turn(2))
    beside = lax.ppermute(jnp.concatenate([below, above]), "xl", NEAR)
    whole = jax.ShapeDtypeStruct((slot_rows, width), bf16)
    first = pl.pallas_call(
        first_kernel,
        out_shape=whole,
        in_specs=[SMEM] + [VMEM] * 4,
        out_specs=ANY,
        scratch_shapes=[pltpu.SemaphoreType.DMA((4,))],
        compiler_params=params,
        name="place_first",
    )(place, own, near, below, above)
    input_grad = pl.pallas_call(
        last_kernel,
        out_shape=whole,
        in_specs=[SMEM, ANY] + [VMEM] * 2,
        out_specs=ANY,
        scratch_shapes=[pltpu.SemaphoreType.DMA((4,))],
        input_output_aliases={1: 0},
        compiler_params=params,
        name="place_last",
    )(place, first, across, beside)
    return (input_grad, down_grad)


def solution(mesh):
    zs = mesh.shape["dp"] // 4
    ys = mesh.shape["rep"] // 2
    finer = Mesh(mesh.devices.reshape(zs, 2, 2, ys, 2), (*DP, *REP))
    in_specs = (P(DP, REP), P(DP, REP), P(REP, None), P(None, REP), P(DP))
    out_specs = (P(DP, None), P(DP, REP))
    return jax.shard_map(
        on_device, mesh=finer, in_specs=in_specs, out_specs=out_specs, check_vma=False
    )
```

```python
import jax
import jax.numpy as jnp
from jax import lax
from jax.experimental import pallas as pl
from jax.experimental.pallas import tpu as pltpu
from jax.sharding import Mesh
from jax.sharding import PartitionSpec as P

DP = ("z", "xh", "core")
REP = ("y", "xl")
RING = ("xh", "xl")
NEAR = [(0, 1), (1, 0)]
FAR = [(0, 3), (3, 0), (1, 2), (2, 1)]
MIXED = [(i, i ^ 1 if i // 2 % 2 == 0 else i ^ 5) for i in range(8)]
ACROSS = [(0, 2), (2, 0), (1, 3), (3, 1)]
VMEM = pl.BlockSpec(memory_space=pltpu.VMEM)
SMEM = pl.BlockSpec(memory_space=pltpu.SMEM)
ANY = pl.BlockSpec(memory_space=pl.ANY)
LIMIT = 12 * 1024 * 1024


def dot(a, b):
    return jnp.dot(a, b, preferred_element_type=jnp.float32)


def split_kernel(place, whole, own, other):
    xl = place[2]
    part = own.shape[0] // 4
    for y in range(4):
        for x, out in ((xl, own), (1 - xl, other)):
            out[y * part:(y + 1) * part, :] = whole[pl.ds(pl.multiple_of((y * 2 + x) * part, 16), part), :]


def live_kernel(place, whole, own, other):
    xl, live = place[2], place[3]
    part = own.shape[0] // 4
    for y in range(4):
        for x, out in ((xl, own), (1 - xl, other)):
            first = pl.multiple_of((y * 2 + x) * part, 16)
            row = first + lax.broadcasted_iota(jnp.int32, (part, out.shape[1]), 0)
            out[y * part:(y + 1) * part, :] = jnp.where(row < live, whole[pl.ds(first, part), :], 0).astype(out.dtype)


def spread_kernel(place, own_set, near_set, out):
    xl = place[2]
    for y in range(out.shape[0]):
        out[y, xl] = own_set[...]
        out[y, 1 - xl] = near_set[...]


def own_kernel(grads, pre, down, out):
    blocks, _, features = grads.shape
    hidden = sum(dot(grads[j], down[j * features:(j + 1) * features, :]) for j in range(blocks))
    out[...] = jnp.where(pre[...] > 0, hidden, 0.0).astype(out.dtype)


def terms_kernel(place, grads, own, pre_far, down_mine, down_other, up_own, up_mine, up_other, terms, up_far):
    core = place[0]
    blocks, features = grads.shape[0], grads.shape[2]
    half = blocks // 2
    units = up_mine.shape[0]
    up_far[pl.ds(pl.multiple_of(core * units, 16), units), :] = up_mine[...]
    up_far[pl.ds(pl.multiple_of((1 - core) * units, 16), units), :] = up_other[...]
    far = sum(
        dot(grads[core * half + j], down_mine[j * features:(j + 1) * features, :]) for j in range(half)
    ) + sum(
        dot(grads[(1 - core) * half + j], down_other[j * features:(j + 1) * features, :]) for j in range(half)
    )
    far = jnp.where(pre_far[...] > 0, far, 0.0).astype(jnp.bfloat16)
    columns = terms.shape[1] // 4
    for i in range(4):
        at = slice(i * columns, (i + 1) * columns)
        terms[:, at] = (dot(own[...], up_own[:, at]) + dot(far, up_far[:, at])).astype(terms.dtype)


def down_kernel(place, grads, pre_own, pre_far, kept, sent):
    core, xh, xl, live = place[0], place[1], place[2], place[3]
    blocks, rows, features = grads.shape
    units = pre_own.shape[1]
    share = kept.shape[2]
    groups = features // (4 * share)
    at = lax.broadcasted_iota(jnp.int32, pre_own.shape, 0)
    part = rows // 4
    row = at + (at // part + xl) * part
    hidden = jnp.concatenate(
        [jnp.where(row < live, jnp.maximum(pre[...], 0), 0).astype(jnp.bfloat16) for pre in (pre_own, pre_far)],
        axis=1,
    )
    for j in range(blocks):
        block = lax.dot_general(
            grads[j], hidden, (((0,), (0,)), ((), ())), preferred_element_type=jnp.float32
        ).astype(kept.dtype)
        for g in range(groups):
            z = j * groups + g
            for h in range(2):
                first = (g * 4 + h * 2) * share
                low = block[first:first + share, :]
                high = block[first + share:first + 2 * share, :]
                mine = jnp.where(core == 0, low, high)
                other = jnp.where(core == 0, high, low)
                for t in range(2):
                    kind = t * 2 + jnp.abs(xh - h)
                    kept[kind, z] = mine[:, t * units:(t + 1) * units]
                    sent[kind, z] = other[:, t * units:(t + 1) * units]


def ring_kernel(own, near, far, across, out):
    total = own[...].astype(jnp.float32) + near[...].astype(jnp.float32)
    out[...] = (total + far[...].astype(jnp.float32) + across[...].astype(jnp.float32)).astype(out.dtype)


def put(place, blocks, out, sems):
    y, xl = place[4], place[2]
    rows = blocks[0][0].shape[0] if len(blocks[0]) == 3 else blocks[0][4]
    ranks = out.shape[0] // (2 * rows)
    running = []
    for i, (block, dy, dx, *rest) in enumerate(blocks):
        at = ((y + dy + ranks) % ranks) * 2 + (1 - xl if dx else xl)
        start = pl.multiple_of(at * rows, 16)
        source = block.at[pl.ds(rest[0], rows)] if rest else block
        copy = pltpu.make_async_copy(source, out.at[pl.ds(start, rows)], sems.at[i])
        copy.start()
        running.append(copy)
    for copy in running:
        copy.wait()


def first_kernel(place, own, near, below, above, out, sems):
    put(place, [(own, 0, 0), (near, 0, 1), (below, -1, 0), (above, 1, 0)], out, sems)


def last_kernel(place, partial, across, beside, out, sems):
    rows = across.shape[0] // 2
    put(
        place,
        [(across, 2, 0, 0, rows), (across, 2, 1, rows, rows), (beside, -1, 1, 0, rows), (beside, 1, 1, rows, rows)],
        out,
        sems,
    )


def own_part(array, index, axis):
    return lax.dynamic_index_in_dim(array, index, axis, keepdims=False)


def on_device(grad_out, pre_act, up_weight, down_weight, slot_counts):
    slot_rows, features = grad_out.shape
    hidden_units = pre_act.shape[1]
    ys, zs = lax.axis_size("y"), lax.axis_size("z")
    reps = 2 * ys
    width = features * reps
    rows = slot_rows // reps
    half_rows = slot_rows // 2
    core, xh, xl, y = (lax.axis_index(a) for a in ("core", "xh", "xl", "y"))
    place = jnp.stack([core, xh, xl, slot_counts[0], y]).astype(jnp.int32)
    bf16 = jnp.bfloat16

    def turn(by):
        return [(i, (i + by) % ys) for i in range(ys)]

    params = pltpu.CompilerParams(vmem_limit_bytes=LIMIT)
    set_shape = jax.ShapeDtypeStruct((half_rows, features), bf16)
    pre_shape = jax.ShapeDtypeStruct((half_rows, hidden_units), bf16)
    own_set, other_set = pl.pallas_call(
        live_kernel,
        out_shape=(set_shape, set_shape),
        in_specs=[SMEM, VMEM],
        out_specs=(VMEM, VMEM),
        compiler_params=params,
        name="live_sets",
    )(place, grad_out)
    pre_own, pre_sent = pl.pallas_call(
        split_kernel,
        out_shape=(pre_shape, pre_shape),
        in_specs=[SMEM, VMEM],
        out_specs=(VMEM, VMEM),
        compiler_params=params,
        name="pre_sets",
    )(place, pre_act)
    near_set = lax.ppermute(other_set, "xl", NEAR)
    grads = pl.pallas_call(
        spread_kernel,
        out_shape=jax.ShapeDtypeStruct((ys, 2, half_rows, features), bf16),
        in_specs=[SMEM] + [VMEM] * 2,
        out_specs=VMEM,
        compiler_params=params,
        name="spread",
    )(place, own_set, near_set)
    grads = lax.all_to_all(grads, "y", 0, 0, tiled=True).reshape(reps, half_rows, features)
    pre_far = lax.ppermute(pre_sent, "xl", NEAR)

    down_mine = lax.ppermute(own_part(down_weight.reshape(2, width // 2, hidden_units), core, 0), RING, FAR)
    up_mine = lax.ppermute(
        own_part(up_weight.reshape(2, hidden_units // 2, width), core, 0), ("xh", "core", "xl"), MIXED
    )
    down_other = lax.ppermute(down_mine, "core", NEAR)
    up_other = lax.ppermute(up_mine, "core", NEAR)

    pre_grad = pl.pallas_call(
        own_kernel,
        out_shape=jax.ShapeDtypeStruct((half_rows, hidden_units), bf16),
        in_specs=[VMEM] * 3,
        out_specs=VMEM,
        compiler_params=pltpu.CompilerParams(vmem_limit_bytes=LIMIT),
        cost_estimate=pl.CostEstimate(
            flops=2 * half_rows * width * hidden_units, bytes_accessed=4 * width * hidden_units, transcendentals=0
        ),
        name="own_grad",
    )(grads, pre_own, down_weight)
    share = width // (4 * zs)
    laid_out = jax.ShapeDtypeStruct((4, zs, share, hidden_units), bf16)
    kept, sent = pl.pallas_call(
        down_kernel,
        out_shape=(laid_out, laid_out),
        in_specs=[SMEM] + [VMEM] * 3,
        out_specs=(VMEM, VMEM),
        compiler_params=pltpu.CompilerParams(vmem_limit_bytes=LIMIT),
        cost_estimate=pl.CostEstimate(
            flops=4 * half_rows * width * hidden_units, bytes_accessed=8 * width * hidden_units, transcendentals=0
        ),
        name="down_terms",
    )(place, grads, pre_own, pre_far)

    pre_later, sent = lax.optimization_barrier((pre_far, sent))
    terms = pl.pallas_call(
        terms_kernel,
        out_shape=jax.ShapeDtypeStruct((half_rows, width), bf16),
        in_specs=[SMEM] + [VMEM] * 8,
        out_specs=VMEM,
        scratch_shapes=[pltpu.VMEM((hidden_units, width), bf16)],
        compiler_params=pltpu.CompilerParams(vmem_limit_bytes=LIMIT),
        cost_estimate=pl.CostEstimate(
            flops=6 * half_rows * width * hidden_units, bytes_accessed=12 * width * hidden_units, transcendentals=0
        ),
        name="terms",
    )(place, grads, pre_grad, pre_later, down_mine, down_other, up_weight, up_mine, up_other)

    f32 = jnp.float32
    came = lax.all_to_all(terms.reshape(ys, rows, width), "y", 0, 0, tiled=True)
    own = sum(came[i].astype(f32) for i in range(ys)).astype(bf16)

    other = lax.ppermute(sent, "core", NEAR)
    chip = [(kept[k].astype(f32) + other[k].astype(f32)) for k in range(4)]
    ring = [
        lax.ppermute(chip[2].astype(bf16), "xl", NEAR),
        lax.ppermute(chip[3].astype(bf16), RING, FAR),
        lax.ppermute(chip[1].astype(bf16), RING, ACROSS),
    ]

    near = lax.ppermute(own, "xl", NEAR)
    below = lax.ppermute(own, "y", turn(1))
    above = lax.ppermute(own, "y", turn(-1))

    own_chip, ring, _ = lax.optimization_barrier((chip[0].astype(bf16), ring, own))
    ring_sum = pl.pallas_call(
        ring_kernel,
        out_shape=jax.ShapeDtypeStruct((zs, share, hidden_units), bf16),
        in_specs=[VMEM] * 4,
        out_specs=VMEM,
        compiler_params=params,
        cost_estimate=pl.CostEstimate(flops=2 * width * hidden_units, bytes_accessed=10 * width * hidden_units, transcendentals=0),
        name="ring_sum",
    )(own_chip, *ring)
    z_terms = lax.all_to_all(ring_sum, "z", 0, 0, tiled=True)
    down_grad = jnp.sum(z_terms.astype(f32), axis=0) / (4 * zs)

    near, below, above = lax.optimization_barrier((near, below, above))
    across = lax.ppermute(jnp.concatenate([own, near]), "y", turn(2))
    beside = lax.ppermute(jnp.concatenate([below, above]), "xl", NEAR)
    whole = jax.ShapeDtypeStruct((slot_rows, width), bf16)
    first = pl.pallas_call(
        first_kernel,
        out_shape=whole,
        in_specs=[SMEM] + [VMEM] * 4,
        out_specs=ANY,
        scratch_shapes=[pltpu.SemaphoreType.DMA((4,))],
        compiler_params=params,
        name="place_first",
    )(place, own, near, below, above)
    input_grad = pl.pallas_call(
        last_kernel,
        out_shape=whole,
        in_specs=[SMEM, ANY] + [VMEM] * 2,
        out_specs=ANY,
        scratch_shapes=[pltpu.SemaphoreType.DMA((4,))],
        input_output_aliases={1: 0},
        compiler_params=params,
        name="place_last",
    )(place, first, across, beside)
    return (input_grad, down_grad)


def solution(mesh):
    zs = mesh.shape["dp"] // 4
    ys = mesh.shape["rep"] // 2
    finer = Mesh(mesh.devices.reshape(zs, 2, 2, ys, 2), (*DP, *REP))
    in_specs = (P(DP, REP), P(DP, REP), P(REP, None), P(None, REP), P(DP))
    out_specs = (P(DP, None), P(DP, REP))
    return jax.shard_map(
        on_device, mesh=finer, in_specs=in_specs, out_specs=out_specs, check_vma=False
    )
```

```python
import jax
import jax.numpy as jnp
from jax import lax
from jax.experimental import pallas as pl
from jax.experimental.pallas import tpu as pltpu
from jax.sharding import Mesh
from jax.sharding import PartitionSpec as P

DP = ("z", "xh", "core")
REP = ("y", "xl")
RING = ("xh", "xl")
NEAR = [(0, 1), (1, 0)]
FAR = [(0, 3), (3, 0), (1, 2), (2, 1)]
MIXED = [(i, i ^ 1 if i // 2 % 2 == 0 else i ^ 5) for i in range(8)]
ACROSS = [(0, 2), (2, 0), (1, 3), (3, 1)]
VMEM = pl.BlockSpec(memory_space=pltpu.VMEM)
SMEM = pl.BlockSpec(memory_space=pltpu.SMEM)
ANY = pl.BlockSpec(memory_space=pl.ANY)
LIMIT = 12 * 1024 * 1024


def dot(a, b):
    return jnp.dot(a, b, preferred_element_type=jnp.float32)


def split_kernel(place, whole, own, other):
    xl = place[2]
    part = own.shape[0] // 4
    for y in range(4):
        for x, out in ((xl, own), (1 - xl, other)):
            out[y * part:(y + 1) * part, :] = whole[pl.ds(pl.multiple_of((y * 2 + x) * part, 16), part), :]


def live_kernel(place, whole, own, other):
    xl, live = place[2], place[3]
    part = own.shape[0] // 4
    for y in range(4):
        for x, out in ((xl, own), (1 - xl, other)):
            first = pl.multiple_of((y * 2 + x) * part, 16)
            row = first + lax.broadcasted_iota(jnp.int32, (part, out.shape[1]), 0)
            out[y * part:(y + 1) * part, :] = jnp.where(row < live, whole[pl.ds(first, part), :], 0).astype(out.dtype)


def spread_kernel(place, own_set, near_set, out):
    xl = place[2]
    for y in range(out.shape[0]):
        out[y, xl] = own_set[...]
        out[y, 1 - xl] = near_set[...]


def own_kernel(grads, pre, down, out):
    blocks, _, features = grads.shape
    hidden = sum(dot(grads[j], down[j * features:(j + 1) * features, :]) for j in range(blocks))
    out[...] = jnp.where(pre[...] > 0, hidden, 0.0).astype(out.dtype)


def terms_kernel(place, grads, own, pre_far, down_mine, down_other, up_own, up_mine, up_other, terms, up_far):
    core = place[0]
    blocks, features = grads.shape[0], grads.shape[2]
    half = blocks // 2
    units = up_mine.shape[0]
    up_far[pl.ds(pl.multiple_of(core * units, 16), units), :] = up_mine[...]
    up_far[pl.ds(pl.multiple_of((1 - core) * units, 16), units), :] = up_other[...]
    far = sum(
        dot(grads[core * half + j], down_mine[j * features:(j + 1) * features, :]) for j in range(half)
    ) + sum(
        dot(grads[(1 - core) * half + j], down_other[j * features:(j + 1) * features, :]) for j in range(half)
    )
    far = jnp.where(pre_far[...] > 0, far, 0.0).astype(jnp.bfloat16)
    columns = terms.shape[1] // 4
    for i in range(4):
        at = slice(i * columns, (i + 1) * columns)
        terms[:, at] = (dot(own[...], up_own[:, at]) + dot(far, up_far[:, at])).astype(terms.dtype)


def down_kernel(place, grads, pre_own, pre_far, kept, sent):
    core, xh, xl, live = place[0], place[1], place[2], place[3]
    blocks, rows, features = grads.shape
    units = pre_own.shape[1]
    share = kept.shape[2]
    groups = features // (4 * share)
    at = lax.broadcasted_iota(jnp.int32, pre_own.shape, 0)
    part = rows // 4
    row = at + (at // part + xl) * part
    hidden = jnp.concatenate(
        [jnp.where(row < live, jnp.maximum(pre[...], 0), 0).astype(jnp.bfloat16) for pre in (pre_own, pre_far)],
        axis=1,
    )
    for j in range(blocks):
        block = lax.dot_general(
            grads[j], hidden, (((0,), (0,)), ((), ())), preferred_element_type=jnp.float32
        ).astype(kept.dtype)
        for g in range(groups):
            z = j * groups + g
            for h in range(2):
                first = (g * 4 + h * 2) * share
                low = block[first:first + share, :]
                high = block[first + share:first + 2 * share, :]
                mine = jnp.where(core == 0, low, high)
                other = jnp.where(core == 0, high, low)
                for t in range(2):
                    kind = t * 2 + jnp.abs(xh - h)
                    kept[kind, z] = mine[:, t * units:(t + 1) * units]
                    sent[kind, z] = other[:, t * units:(t + 1) * units]


def ring_kernel(own, near, far, across, out):
    total = own[...].astype(jnp.float32) + near[...].astype(jnp.float32)
    out[...] = (total + far[...].astype(jnp.float32) + across[...].astype(jnp.float32)).astype(out.dtype)


def put(place, blocks, out, sems):
    y, xl = place[4], place[2]
    rows = blocks[0][0].shape[0] if len(blocks[0]) == 3 else blocks[0][4]
    ranks = out.shape[0] // (2 * rows)
    running = []
    for i, (block, dy, dx, *rest) in enumerate(blocks):
        at = ((y + dy + ranks) % ranks) * 2 + (1 - xl if dx else xl)
        start = pl.multiple_of(at * rows, 16)
        source = block.at[pl.ds(rest[0], rows)] if rest else block
        copy = pltpu.make_async_copy(source, out.at[pl.ds(start, rows)], sems.at[i])
        copy.start()
        running.append(copy)
    for copy in running:
        copy.wait()


def first_kernel(place, own, near, below, above, out, sems):
    put(place, [(own, 0, 0), (near, 0, 1), (below, -1, 0), (above, 1, 0)], out, sems)


def across_kernel(place, partial, across, out, sems):
    rows = across.shape[0] // 2
    put(place, [(across, 2, 0, 0, rows), (across, 2, 1, rows, rows)], out, sems)


def beside_kernel(place, partial, beside, out, sems):
    rows = beside.shape[0] // 2
    put(place, [(beside, -1, 1, 0, rows), (beside, 1, 1, rows, rows)], out, sems)


def own_part(array, index, axis):
    return lax.dynamic_index_in_dim(array, index, axis, keepdims=False)


def on_device(grad_out, pre_act, up_weight, down_weight, slot_counts):
    slot_rows, features = grad_out.shape
    hidden_units = pre_act.shape[1]
    ys, zs = lax.axis_size("y"), lax.axis_size("z")
    reps = 2 * ys
    width = features * reps
    rows = slot_rows // reps
    half_rows = slot_rows // 2
    core, xh, xl, y = (lax.axis_index(a) for a in ("core", "xh", "xl", "y"))
    place = jnp.stack([core, xh, xl, slot_counts[0], y]).astype(jnp.int32)
    bf16 = jnp.bfloat16

    def turn(by):
        return [(i, (i + by) % ys) for i in range(ys)]

    params = pltpu.CompilerParams(vmem_limit_bytes=LIMIT)
    set_shape = jax.ShapeDtypeStruct((half_rows, features), bf16)
    pre_shape = jax.ShapeDtypeStruct((half_rows, hidden_units), bf16)
    own_set, other_set = pl.pallas_call(
        live_kernel,
        out_shape=(set_shape, set_shape),
        in_specs=[SMEM, VMEM],
        out_specs=(VMEM, VMEM),
        compiler_params=params,
        name="live_sets",
    )(place, grad_out)
    pre_own, pre_sent = pl.pallas_call(
        split_kernel,
        out_shape=(pre_shape, pre_shape),
        in_specs=[SMEM, VMEM],
        out_specs=(VMEM, VMEM),
        compiler_params=params,
        name="pre_sets",
    )(place, pre_act)
    near_set = lax.ppermute(other_set, "xl", NEAR)
    grads = pl.pallas_call(
        spread_kernel,
        out_shape=jax.ShapeDtypeStruct((ys, 2, half_rows, features), bf16),
        in_specs=[SMEM] + [VMEM] * 2,
        out_specs=VMEM,
        compiler_params=params,
        name="spread",
    )(place, own_set, near_set)
    grads = lax.all_to_all(grads, "y", 0, 0, tiled=True).reshape(reps, half_rows, features)
    pre_far = lax.ppermute(pre_sent, "xl", NEAR)

    down_mine = lax.ppermute(own_part(down_weight.reshape(2, width // 2, hidden_units), core, 0), RING, FAR)
    up_mine = lax.ppermute(
        own_part(up_weight.reshape(2, hidden_units // 2, width), core, 0), ("xh", "core", "xl"), MIXED
    )
    down_other = lax.ppermute(down_mine, "core", NEAR)
    up_other = lax.ppermute(up_mine, "core", NEAR)

    pre_grad = pl.pallas_call(
        own_kernel,
        out_shape=jax.ShapeDtypeStruct((half_rows, hidden_units), bf16),
        in_specs=[VMEM] * 3,
        out_specs=VMEM,
        compiler_params=pltpu.CompilerParams(vmem_limit_bytes=LIMIT),
        cost_estimate=pl.CostEstimate(
            flops=2 * half_rows * width * hidden_units, bytes_accessed=4 * width * hidden_units, transcendentals=0
        ),
        name="own_grad",
    )(grads, pre_own, down_weight)
    share = width // (4 * zs)
    laid_out = jax.ShapeDtypeStruct((4, zs, share, hidden_units), bf16)
    kept, sent = pl.pallas_call(
        down_kernel,
        out_shape=(laid_out, laid_out),
        in_specs=[SMEM] + [VMEM] * 3,
        out_specs=(VMEM, VMEM),
        compiler_params=pltpu.CompilerParams(vmem_limit_bytes=LIMIT),
        cost_estimate=pl.CostEstimate(
            flops=4 * half_rows * width * hidden_units, bytes_accessed=8 * width * hidden_units, transcendentals=0
        ),
        name="down_terms",
    )(place, grads, pre_own, pre_far)

    pre_later, sent = lax.optimization_barrier((pre_far, sent))
    terms = pl.pallas_call(
        terms_kernel,
        out_shape=jax.ShapeDtypeStruct((half_rows, width), bf16),
        in_specs=[SMEM] + [VMEM] * 8,
        out_specs=VMEM,
        scratch_shapes=[pltpu.VMEM((hidden_units, width), bf16)],
        compiler_params=pltpu.CompilerParams(vmem_limit_bytes=LIMIT),
        cost_estimate=pl.CostEstimate(
            flops=6 * half_rows * width * hidden_units, bytes_accessed=12 * width * hidden_units, transcendentals=0
        ),
        name="terms",
    )(place, grads, pre_grad, pre_later, down_mine, down_other, up_weight, up_mine, up_other)

    f32 = jnp.float32
    came = lax.all_to_all(terms.reshape(ys, rows, width), "y", 0, 0, tiled=True)
    own = sum(came[i].astype(f32) for i in range(ys)).astype(bf16)

    other = lax.ppermute(sent, "core", NEAR)
    chip = [(kept[k].astype(f32) + other[k].astype(f32)) for k in range(4)]
    ring = [
        lax.ppermute(chip[2].astype(bf16), "xl", NEAR),
        lax.ppermute(chip[3].astype(bf16), RING, FAR),
        lax.ppermute(chip[1].astype(bf16), RING, ACROSS),
    ]

    near = lax.ppermute(own, "xl", NEAR)
    below = lax.ppermute(own, "y", turn(1))
    above = lax.ppermute(own, "y", turn(-1))

    own_chip, ring, _ = lax.optimization_barrier((chip[0].astype(bf16), ring, own))
    ring_sum = pl.pallas_call(
        ring_kernel,
        out_shape=jax.ShapeDtypeStruct((zs, share, hidden_units), bf16),
        in_specs=[VMEM] * 4,
        out_specs=VMEM,
        compiler_params=params,
        cost_estimate=pl.CostEstimate(flops=2 * width * hidden_units, bytes_accessed=10 * width * hidden_units, transcendentals=0),
        name="ring_sum",
    )(own_chip, *ring)
    z_terms = lax.all_to_all(ring_sum, "z", 0, 0, tiled=True)
    down_grad = jnp.sum(z_terms.astype(f32), axis=0) / (4 * zs)

    near, below, above = lax.optimization_barrier((near, below, above))
    across = lax.ppermute(jnp.concatenate([own, near]), "y", turn(2))
    beside = lax.ppermute(jnp.concatenate([below, above]), "xl", NEAR)
    whole = jax.ShapeDtypeStruct((slot_rows, width), bf16)
    first = pl.pallas_call(
        first_kernel,
        out_shape=whole,
        in_specs=[SMEM] + [VMEM] * 4,
        out_specs=ANY,
        scratch_shapes=[pltpu.SemaphoreType.DMA((4,))],
        compiler_params=params,
        name="place_first",
    )(place, own, near, below, above)
    input_grad = first
    for kernel, pair, name in ((across_kernel, across, "place_across"), (beside_kernel, beside, "place_beside")):
        input_grad = pl.pallas_call(
            kernel,
            out_shape=whole,
            in_specs=[SMEM, ANY, VMEM],
            out_specs=ANY,
            scratch_shapes=[pltpu.SemaphoreType.DMA((2,))],
            input_output_aliases={1: 0},
            compiler_params=pltpu.CompilerParams(vmem_limit_bytes=LIMIT),
            name=name,
        )(place, input_grad, pair)
    return (input_grad, down_grad)


def solution(mesh):
    zs = mesh.shape["dp"] // 4
    ys = mesh.shape["rep"] // 2
    finer = Mesh(mesh.devices.reshape(zs, 2, 2, ys, 2), (*DP, *REP))
    in_specs = (P(DP, REP), P(DP, REP), P(REP, None), P(None, REP), P(DP))
    out_specs = (P(DP, None), P(DP, REP))
    return jax.shard_map(
        on_device, mesh=finer, in_specs=in_specs, out_specs=out_specs, check_vma=False
    )
```

```python
import jax
import jax.numpy as jnp
from jax import lax
from jax.experimental import pallas as pl
from jax.experimental.pallas import tpu as pltpu
from jax.sharding import Mesh
from jax.sharding import PartitionSpec as P

DP = ("z", "xh", "core")
REP = ("y", "xl")
RING = ("xh", "xl")
NEAR = [(0, 1), (1, 0)]
FAR = [(0, 3), (3, 0), (1, 2), (2, 1)]
MIXED = [(i, i ^ 1 if i // 2 % 2 == 0 else i ^ 5) for i in range(8)]
ACROSS = [(0, 2), (2, 0), (1, 3), (3, 1)]
VMEM = pl.BlockSpec(memory_space=pltpu.VMEM)
SMEM = pl.BlockSpec(memory_space=pltpu.SMEM)
ANY = pl.BlockSpec(memory_space=pl.ANY)
LIMIT = 12 * 1024 * 1024


def dot(a, b):
    return jnp.dot(a, b, preferred_element_type=jnp.float32)


def split_kernel(place, whole, own, other):
    xl = place[2]
    part = own.shape[0] // 4
    for y in range(4):
        for x, out in ((xl, own), (1 - xl, other)):
            out[y * part:(y + 1) * part, :] = whole[pl.ds(pl.multiple_of((y * 2 + x) * part, 16), part), :]


def live_kernel(place, whole, own, other):
    xl, live = place[2], place[3]
    part = own.shape[0] // 4
    for y in range(4):
        for x, out in ((xl, own), (1 - xl, other)):
            first = pl.multiple_of((y * 2 + x) * part, 16)
            row = first + lax.broadcasted_iota(jnp.int32, (part, out.shape[1]), 0)
            out[y * part:(y + 1) * part, :] = jnp.where(row < live, whole[pl.ds(first, part), :], 0).astype(out.dtype)


def own_spread_kernel(place, own_set, out):
    for y in range(out.shape[0]):
        out[y, place[2]] = own_set[...]


def near_spread_kernel(place, partial, near_set, out, sems):
    copies = [
        pltpu.make_async_copy(near_set, out.at[y, 1 - place[2]], sems.at[y]) for y in range(out.shape[0])
    ]
    for copy in copies:
        copy.start()
    for copy in copies:
        copy.wait()


def own_kernel(grads, pre, down, out):
    blocks, _, features = grads.shape
    hidden = sum(dot(grads[j], down[j * features:(j + 1) * features, :]) for j in range(blocks))
    out[...] = jnp.where(pre[...] > 0, hidden, 0.0).astype(out.dtype)


def terms_kernel(place, grads, own, pre_far, down_mine, down_other, up_own, up_mine, up_other, terms, up_far):
    core = place[0]
    blocks, features = grads.shape[0], grads.shape[2]
    half = blocks // 2
    units = up_mine.shape[0]
    up_far[pl.ds(pl.multiple_of(core * units, 16), units), :] = up_mine[...]
    up_far[pl.ds(pl.multiple_of((1 - core) * units, 16), units), :] = up_other[...]
    far = sum(
        dot(grads[core * half + j], down_mine[j * features:(j + 1) * features, :]) for j in range(half)
    ) + sum(
        dot(grads[(1 - core) * half + j], down_other[j * features:(j + 1) * features, :]) for j in range(half)
    )
    far = jnp.where(pre_far[...] > 0, far, 0.0).astype(jnp.bfloat16)
    columns = terms.shape[1] // 4
    for i in range(4):
        at = slice(i * columns, (i + 1) * columns)
        terms[:, at] = (dot(own[...], up_own[:, at]) + dot(far, up_far[:, at])).astype(terms.dtype)


def down_kernel(place, grads, pre_own, pre_far, kept, sent):
    core, xh, xl, live = place[0], place[1], place[2], place[3]
    blocks, rows, features = grads.shape
    units = pre_own.shape[1]
    share = kept.shape[2]
    groups = features // (4 * share)
    at = lax.broadcasted_iota(jnp.int32, pre_own.shape, 0)
    part = rows // 4
    row = at + (at // part + xl) * part
    hidden = jnp.concatenate(
        [jnp.where(row < live, jnp.maximum(pre[...], 0), 0).astype(jnp.bfloat16) for pre in (pre_own, pre_far)],
        axis=1,
    )
    for j in range(blocks):
        block = lax.dot_general(
            grads[j], hidden, (((0,), (0,)), ((), ())), preferred_element_type=jnp.float32
        ).astype(kept.dtype)
        for g in range(groups):
            z = j * groups + g
            for h in range(2):
                first = (g * 4 + h * 2) * share
                low = block[first:first + share, :]
                high = block[first + share:first + 2 * share, :]
                mine = jnp.where(core == 0, low, high)
                other = jnp.where(core == 0, high, low)
                for t in range(2):
                    kind = t * 2 + jnp.abs(xh - h)
                    kept[kind, z] = mine[:, t * units:(t + 1) * units]
                    sent[kind, z] = other[:, t * units:(t + 1) * units]


def ring_kernel(own, near, far, across, out):
    total = own[...].astype(jnp.float32) + near[...].astype(jnp.float32)
    out[...] = (total + far[...].astype(jnp.float32) + across[...].astype(jnp.float32)).astype(out.dtype)


def put(place, blocks, out, sems):
    y, xl = place[4], place[2]
    rows = blocks[0][0].shape[0] if len(blocks[0]) == 3 else blocks[0][4]
    ranks = out.shape[0] // (2 * rows)
    running = []
    for i, (block, dy, dx, *rest) in enumerate(blocks):
        at = ((y + dy + ranks) % ranks) * 2 + (1 - xl if dx else xl)
        start = pl.multiple_of(at * rows, 16)
        source = block.at[pl.ds(rest[0], rows)] if rest else block
        copy = pltpu.make_async_copy(source, out.at[pl.ds(start, rows)], sems.at[i])
        copy.start()
        running.append(copy)
    for copy in running:
        copy.wait()


def first_kernel(place, own, near, below, above, out, sems):
    put(place, [(own, 0, 0), (near, 0, 1), (below, -1, 0), (above, 1, 0)], out, sems)


def across_kernel(place, partial, across, out, sems):
    rows = across.shape[0] // 2
    put(place, [(across, 2, 0, 0, rows), (across, 2, 1, rows, rows)], out, sems)


def beside_kernel(place, partial, beside, out, sems):
    rows = beside.shape[0] // 2
    put(place, [(beside, -1, 1, 0, rows), (beside, 1, 1, rows, rows)], out, sems)


def own_part(array, index, axis):
    return lax.dynamic_index_in_dim(array, index, axis, keepdims=False)


def on_device(grad_out, pre_act, up_weight, down_weight, slot_counts):
    slot_rows, features = grad_out.shape
    hidden_units = pre_act.shape[1]
    ys, zs = lax.axis_size("y"), lax.axis_size("z")
    reps = 2 * ys
    width = features * reps
    rows = slot_rows // reps
    half_rows = slot_rows // 2
    core, xh, xl, y = (lax.axis_index(a) for a in ("core", "xh", "xl", "y"))
    place = jnp.stack([core, xh, xl, slot_counts[0], y]).astype(jnp.int32)
    bf16 = jnp.bfloat16

    def turn(by):
        return [(i, (i + by) % ys) for i in range(ys)]

    params = pltpu.CompilerParams(vmem_limit_bytes=LIMIT)
    set_shape = jax.ShapeDtypeStruct((half_rows, features), bf16)
    pre_shape = jax.ShapeDtypeStruct((half_rows, hidden_units), bf16)
    own_set, other_set = pl.pallas_call(
        live_kernel,
        out_shape=(set_shape, set_shape),
        in_specs=[SMEM, VMEM],
        out_specs=(VMEM, VMEM),
        compiler_params=params,
        name="live_sets",
    )(place, grad_out)
    pre_own, pre_sent = pl.pallas_call(
        split_kernel,
        out_shape=(pre_shape, pre_shape),
        in_specs=[SMEM, VMEM],
        out_specs=(VMEM, VMEM),
        compiler_params=params,
        name="pre_sets",
    )(place, pre_act)
    near_set = lax.ppermute(other_set, "xl", NEAR)
    spread = jax.ShapeDtypeStruct((ys, 2, half_rows, features), bf16)
    grads = pl.pallas_call(
        own_spread_kernel,
        out_shape=spread,
        in_specs=[SMEM, VMEM],
        out_specs=VMEM,
        compiler_params=pltpu.CompilerParams(vmem_limit_bytes=LIMIT),
        name="spread_own",
    )(place, own_set)
    grads = pl.pallas_call(
        near_spread_kernel,
        out_shape=spread,
        in_specs=[SMEM, ANY, VMEM],
        out_specs=ANY,
        scratch_shapes=[pltpu.SemaphoreType.DMA((ys,))],
        input_output_aliases={1: 0},
        compiler_params=pltpu.CompilerParams(vmem_limit_bytes=LIMIT),
        name="spread_near",
    )(place, grads, near_set)
    grads = lax.all_to_all(grads, "y", 0, 0, tiled=True).reshape(reps, half_rows, features)
    pre_far = lax.ppermute(pre_sent, "xl", NEAR)

    down_mine = lax.ppermute(own_part(down_weight.reshape(2, width // 2, hidden_units), core, 0), RING, FAR)
    up_mine = lax.ppermute(
        own_part(up_weight.reshape(2, hidden_units // 2, width), core, 0), ("xh", "core", "xl"), MIXED
    )
    down_other = lax.ppermute(down_mine, "core", NEAR)
    up_other = lax.ppermute(up_mine, "core", NEAR)

    pre_grad = pl.pallas_call(
        own_kernel,
        out_shape=jax.ShapeDtypeStruct((half_rows, hidden_units), bf16),
        in_specs=[VMEM] * 3,
        out_specs=VMEM,
        compiler_params=pltpu.CompilerParams(vmem_limit_bytes=LIMIT),
        cost_estimate=pl.CostEstimate(
            flops=2 * half_rows * width * hidden_units, bytes_accessed=4 * width * hidden_units, transcendentals=0
        ),
        name="own_grad",
    )(grads, pre_own, down_weight)
    share = width // (4 * zs)
    laid_out = jax.ShapeDtypeStruct((4, zs, share, hidden_units), bf16)
    kept, sent = pl.pallas_call(
        down_kernel,
        out_shape=(laid_out, laid_out),
        in_specs=[SMEM] + [VMEM] * 3,
        out_specs=(VMEM, VMEM),
        compiler_params=pltpu.CompilerParams(vmem_limit_bytes=LIMIT),
        cost_estimate=pl.CostEstimate(
            flops=4 * half_rows * width * hidden_units, bytes_accessed=8 * width * hidden_units, transcendentals=0
        ),
        name="down_terms",
    )(place, grads, pre_own, pre_far)

    pre_later, sent = lax.optimization_barrier((pre_far, sent))
    terms = pl.pallas_call(
        terms_kernel,
        out_shape=jax.ShapeDtypeStruct((half_rows, width), bf16),
        in_specs=[SMEM] + [VMEM] * 8,
        out_specs=VMEM,
        scratch_shapes=[pltpu.VMEM((hidden_units, width), bf16)],
        compiler_params=pltpu.CompilerParams(vmem_limit_bytes=LIMIT),
        cost_estimate=pl.CostEstimate(
            flops=6 * half_rows * width * hidden_units, bytes_accessed=12 * width * hidden_units, transcendentals=0
        ),
        name="terms",
    )(place, grads, pre_grad, pre_later, down_mine, down_other, up_weight, up_mine, up_other)

    f32 = jnp.float32
    came = lax.all_to_all(terms.reshape(ys, rows, width), "y", 0, 0, tiled=True)
    own = sum(came[i].astype(f32) for i in range(ys)).astype(bf16)

    other = lax.ppermute(sent, "core", NEAR)
    chip = [(kept[k].astype(f32) + other[k].astype(f32)) for k in range(4)]
    ring = [
        lax.ppermute(chip[2].astype(bf16), "xl", NEAR),
        lax.ppermute(chip[3].astype(bf16), RING, FAR),
        lax.ppermute(chip[1].astype(bf16), RING, ACROSS),
    ]

    near = lax.ppermute(own, "xl", NEAR)
    below = lax.ppermute(own, "y", turn(1))
    above = lax.ppermute(own, "y", turn(-1))

    own_chip, ring, _ = lax.optimization_barrier((chip[0].astype(bf16), ring, own))
    ring_sum = pl.pallas_call(
        ring_kernel,
        out_shape=jax.ShapeDtypeStruct((zs, share, hidden_units), bf16),
        in_specs=[VMEM] * 4,
        out_specs=VMEM,
        compiler_params=params,
        cost_estimate=pl.CostEstimate(flops=2 * width * hidden_units, bytes_accessed=10 * width * hidden_units, transcendentals=0),
        name="ring_sum",
    )(own_chip, *ring)
    z_terms = lax.all_to_all(ring_sum, "z", 0, 0, tiled=True)
    down_grad = jnp.sum(z_terms.astype(f32), axis=0) / (4 * zs)

    near, below, above = lax.optimization_barrier((near, below, above))
    across = lax.ppermute(jnp.concatenate([own, near]), "y", turn(2))
    beside = lax.ppermute(jnp.concatenate([below, above]), "xl", NEAR)
    whole = jax.ShapeDtypeStruct((slot_rows, width), bf16)
    first = pl.pallas_call(
        first_kernel,
        out_shape=whole,
        in_specs=[SMEM] + [VMEM] * 4,
        out_specs=ANY,
        scratch_shapes=[pltpu.SemaphoreType.DMA((4,))],
        compiler_params=params,
        name="place_first",
    )(place, own, near, below, above)
    input_grad = first
    for kernel, pair, name in ((across_kernel, across, "place_across"), (beside_kernel, beside, "place_beside")):
        input_grad = pl.pallas_call(
            kernel,
            out_shape=whole,
            in_specs=[SMEM, ANY, VMEM],
            out_specs=ANY,
            scratch_shapes=[pltpu.SemaphoreType.DMA((2,))],
            input_output_aliases={1: 0},
            compiler_params=pltpu.CompilerParams(vmem_limit_bytes=LIMIT),
            name=name,
        )(place, input_grad, pair)
    return (input_grad, down_grad)


def solution(mesh):
    zs = mesh.shape["dp"] // 4
    ys = mesh.shape["rep"] // 2
    finer = Mesh(mesh.devices.reshape(zs, 2, 2, ys, 2), (*DP, *REP))
    in_specs = (P(DP, REP), P(DP, REP), P(REP, None), P(None, REP), P(DP))
    out_specs = (P(DP, None), P(DP, REP))
    return jax.shard_map(
        on_device, mesh=finer, in_specs=in_specs, out_specs=out_specs, check_vma=False
    )
```

```python
import jax
import jax.numpy as jnp
from jax import lax
from jax.experimental import pallas as pl
from jax.experimental.pallas import tpu as pltpu
from jax.sharding import Mesh
from jax.sharding import PartitionSpec as P

DP = ("z", "xh", "core")
REP = ("y", "xl")
RING = ("xh", "xl")
NEAR = [(0, 1), (1, 0)]
FAR = [(0, 3), (3, 0), (1, 2), (2, 1)]
MIXED = [(i, i ^ 1 if i // 2 % 2 == 0 else i ^ 5) for i in range(8)]
ACROSS = [(0, 2), (2, 0), (1, 3), (3, 1)]
VMEM = pl.BlockSpec(memory_space=pltpu.VMEM)
SMEM = pl.BlockSpec(memory_space=pltpu.SMEM)
ANY = pl.BlockSpec(memory_space=pl.ANY)
LIMIT = 12 * 1024 * 1024


def dot(a, b):
    return jnp.dot(a, b, preferred_element_type=jnp.float32)


def split_kernel(place, whole, own, other):
    xl = place[2]
    part = own.shape[0] // 4
    for y in range(4):
        for x, out in ((xl, own), (1 - xl, other)):
            out[y * part:(y + 1) * part, :] = whole[pl.ds(pl.multiple_of((y * 2 + x) * part, 16), part), :]


def live_kernel(place, whole, own, other):
    xl, live = place[2], place[3]
    part = own.shape[0] // 4
    for y in range(4):
        for x, out in ((xl, own), (1 - xl, other)):
            first = pl.multiple_of((y * 2 + x) * part, 16)
            row = first + lax.broadcasted_iota(jnp.int32, (part, out.shape[1]), 0)
            out[y * part:(y + 1) * part, :] = jnp.where(row < live, whole[pl.ds(first, part), :], 0).astype(out.dtype)


def spread_kernel(place, own_set, near_set, out):
    xl = place[2]
    for y in range(out.shape[0]):
        out[y, xl] = own_set[...]
        out[y, 1 - xl] = near_set[...]


def own_kernel(grads, pre, down, out):
    blocks, _, features = grads.shape
    hidden = sum(dot(grads[j], down[j * features:(j + 1) * features, :]) for j in range(blocks))
    out[...] = jnp.where(pre[...] > 0, hidden, 0.0).astype(out.dtype)


def terms_kernel(place, grads, own, pre_far, down_mine, down_other, up_own, up_mine, up_other, terms, up_far):
    core = place[0]
    blocks, features = grads.shape[0], grads.shape[2]
    half = blocks // 2
    units = up_mine.shape[0]
    up_far[pl.ds(pl.multiple_of(core * units, 16), units), :] = up_mine[...]
    up_far[pl.ds(pl.multiple_of((1 - core) * units, 16), units), :] = up_other[...]
    far = sum(
        dot(grads[core * half + j], down_mine[j * features:(j + 1) * features, :]) for j in range(half)
    ) + sum(
        dot(grads[(1 - core) * half + j], down_other[j * features:(j + 1) * features, :]) for j in range(half)
    )
    far = jnp.where(pre_far[...] > 0, far, 0.0).astype(jnp.bfloat16)
    columns = terms.shape[1] // 4
    for i in range(4):
        at = slice(i * columns, (i + 1) * columns)
        terms[:, at] = (dot(own[...], up_own[:, at]) + dot(far, up_far[:, at])).astype(terms.dtype)


def down_kernel(place, grads, pre_own, pre_far, kept, sent):
    core, xh, xl, live = place[0], place[1], place[2], place[3]
    blocks, rows, features = grads.shape
    units = pre_own.shape[1]
    share = kept.shape[2]
    groups = features // (4 * share)
    at = lax.broadcasted_iota(jnp.int32, pre_own.shape, 0)
    part = rows // 4
    row = at + (at // part + xl) * part
    hidden = jnp.concatenate(
        [jnp.where(row < live, jnp.maximum(pre[...], 0), 0).astype(jnp.bfloat16) for pre in (pre_own, pre_far)],
        axis=1,
    )
    for j in range(blocks):
        block = lax.dot_general(
            grads[j], hidden, (((0,), (0,)), ((), ())), preferred_element_type=jnp.float32
        ).astype(kept.dtype)
        for g in range(groups):
            z = j * groups + g
            for h in range(2):
                first = (g * 4 + h * 2) * share
                low = block[first:first + share, :]
                high = block[first + share:first + 2 * share, :]
                mine = jnp.where(core == 0, low, high)
                other = jnp.where(core == 0, high, low)
                for t in range(2):
                    kind = t * 2 + jnp.abs(xh - h)
                    kept[kind, z] = mine[:, t * units:(t + 1) * units]
                    sent[kind, z] = other[:, t * units:(t + 1) * units]


def ring_kernel(own, near, far, across, out):
    total = own[...].astype(jnp.float32) + near[...].astype(jnp.float32)
    out[...] = (total + far[...].astype(jnp.float32) + across[...].astype(jnp.float32)).astype(out.dtype)


def put(place, blocks, out, sems):
    y, xl = place[4], place[2]
    rows = blocks[0][0].shape[0] if len(blocks[0]) == 3 else blocks[0][4]
    ranks = out.shape[0] // (2 * rows)
    running = []
    for i, (block, dy, dx, *rest) in enumerate(blocks):
        at = ((y + dy + ranks) % ranks) * 2 + (1 - xl if dx else xl)
        start = pl.multiple_of(at * rows, 16)
        source = block.at[pl.ds(rest[0], rows)] if rest else block
        copy = pltpu.make_async_copy(source, out.at[pl.ds(start, rows)], sems.at[i])
        copy.start()
        running.append(copy)
    for copy in running:
        copy.wait()


def first_kernel(place, own, near, below, above, out, sems):
    put(place, [(own, 0, 0), (near, 0, 1), (below, -1, 0), (above, 1, 0)], out, sems)


def last_kernel(place, partial, beside, across, out, sems):
    rows = across.shape[0] // 2
    put(
        place,
        [(across, 2, 0, 0, rows), (across, 2, 1, rows, rows), (beside, -1, 1, 0, rows), (beside, 1, 1, rows, rows)],
        out,
        sems,
    )


def own_part(array, index, axis):
    return lax.dynamic_index_in_dim(array, index, axis, keepdims=False)


def on_device(grad_out, pre_act, up_weight, down_weight, slot_counts):
    slot_rows, features = grad_out.shape
    hidden_units = pre_act.shape[1]
    ys, zs = lax.axis_size("y"), lax.axis_size("z")
    reps = 2 * ys
    width = features * reps
    rows = slot_rows // reps
    half_rows = slot_rows // 2
    core, xh, xl, y = (lax.axis_index(a) for a in ("core", "xh", "xl", "y"))
    place = jnp.stack([core, xh, xl, slot_counts[0], y]).astype(jnp.int32)
    bf16 = jnp.bfloat16

    def turn(by):
        return [(i, (i + by) % ys) for i in range(ys)]

    params = pltpu.CompilerParams(vmem_limit_bytes=LIMIT)
    set_shape = jax.ShapeDtypeStruct((half_rows, features), bf16)
    pre_shape = jax.ShapeDtypeStruct((half_rows, hidden_units), bf16)
    own_set, other_set = pl.pallas_call(
        live_kernel,
        out_shape=(set_shape, set_shape),
        in_specs=[SMEM, VMEM],
        out_specs=(VMEM, VMEM),
        compiler_params=params,
        name="live_sets",
    )(place, grad_out)
    pre_own, pre_sent = pl.pallas_call(
        split_kernel,
        out_shape=(pre_shape, pre_shape),
        in_specs=[SMEM, VMEM],
        out_specs=(VMEM, VMEM),
        compiler_params=params,
        name="pre_sets",
    )(place, pre_act)
    near_set = lax.ppermute(other_set, "xl", NEAR)
    grads = pl.pallas_call(
        spread_kernel,
        out_shape=jax.ShapeDtypeStruct((ys, 2, half_rows, features), bf16),
        in_specs=[SMEM] + [VMEM] * 2,
        out_specs=VMEM,
        compiler_params=params,
        name="spread",
    )(place, own_set, near_set)
    grads = lax.all_to_all(grads, "y", 0, 0, tiled=True).reshape(reps, half_rows, features)
    pre_far = lax.ppermute(pre_sent, "xl", NEAR)

    down_mine = lax.ppermute(own_part(down_weight.reshape(2, width // 2, hidden_units), core, 0), RING, FAR)
    up_mine = lax.ppermute(
        own_part(up_weight.reshape(2, hidden_units // 2, width), core, 0), ("xh", "core", "xl"), MIXED
    )
    down_other = lax.ppermute(down_mine, "core", NEAR)
    up_other = lax.ppermute(up_mine, "core", NEAR)

    pre_grad = pl.pallas_call(
        own_kernel,
        out_shape=jax.ShapeDtypeStruct((half_rows, hidden_units), bf16),
        in_specs=[VMEM] * 3,
        out_specs=VMEM,
        compiler_params=pltpu.CompilerParams(vmem_limit_bytes=LIMIT),
        cost_estimate=pl.CostEstimate(
            flops=2 * half_rows * width * hidden_units, bytes_accessed=4 * width * hidden_units, transcendentals=0
        ),
        name="own_grad",
    )(grads, pre_own, down_weight)
    share = width // (4 * zs)
    laid_out = jax.ShapeDtypeStruct((4, zs, share, hidden_units), bf16)
    kept, sent = pl.pallas_call(
        down_kernel,
        out_shape=(laid_out, laid_out),
        in_specs=[SMEM] + [VMEM] * 3,
        out_specs=(VMEM, VMEM),
        compiler_params=pltpu.CompilerParams(vmem_limit_bytes=LIMIT),
        cost_estimate=pl.CostEstimate(
            flops=4 * half_rows * width * hidden_units, bytes_accessed=8 * width * hidden_units, transcendentals=0
        ),
        name="down_terms",
    )(place, grads, pre_own, pre_far)

    pre_later, sent = lax.optimization_barrier((pre_far, sent))
    terms = pl.pallas_call(
        terms_kernel,
        out_shape=jax.ShapeDtypeStruct((half_rows, width), bf16),
        in_specs=[SMEM] + [VMEM] * 8,
        out_specs=VMEM,
        scratch_shapes=[pltpu.VMEM((hidden_units, width), bf16)],
        compiler_params=pltpu.CompilerParams(vmem_limit_bytes=LIMIT),
        cost_estimate=pl.CostEstimate(
            flops=6 * half_rows * width * hidden_units, bytes_accessed=12 * width * hidden_units, transcendentals=0
        ),
        name="terms",
    )(place, grads, pre_grad, pre_later, down_mine, down_other, up_weight, up_mine, up_other)

    f32 = jnp.float32
    came = lax.all_to_all(terms.reshape(ys, rows, width), "y", 0, 0, tiled=True)
    own = sum(came[i].astype(f32) for i in range(ys)).astype(bf16)

    other = lax.ppermute(sent, "core", NEAR)
    chip = [(kept[k].astype(f32) + other[k].astype(f32)) for k in range(4)]
    ring = [
        lax.ppermute(chip[2].astype(bf16), "xl", NEAR),
        lax.ppermute(chip[3].astype(bf16), RING, FAR),
        lax.ppermute(chip[1].astype(bf16), RING, ACROSS),
    ]

    near = lax.ppermute(own, "xl", NEAR)
    below = lax.ppermute(own, "y", turn(1))
    above = lax.ppermute(own, "y", turn(-1))

    own_chip, ring, _ = lax.optimization_barrier((chip[0].astype(bf16), ring, own))
    ring_sum = pl.pallas_call(
        ring_kernel,
        out_shape=jax.ShapeDtypeStruct((zs, share, hidden_units), bf16),
        in_specs=[VMEM] * 4,
        out_specs=VMEM,
        compiler_params=params,
        cost_estimate=pl.CostEstimate(flops=2 * width * hidden_units, bytes_accessed=10 * width * hidden_units, transcendentals=0),
        name="ring_sum",
    )(own_chip, *ring)
    z_terms = lax.all_to_all(ring_sum, "z", 0, 0, tiled=True)
    down_grad = jnp.sum(z_terms.astype(f32), axis=0) / (4 * zs)

    near, below, above = lax.optimization_barrier((near, below, above))
    across = lax.ppermute(jnp.concatenate([own, near]), "y", turn(2))
    beside = lax.ppermute(jnp.concatenate([below, above]), "xl", NEAR)
    whole = jax.ShapeDtypeStruct((slot_rows, width), bf16)
    first = pl.pallas_call(
        first_kernel,
        out_shape=whole,
        in_specs=[SMEM] + [VMEM] * 4,
        out_specs=ANY,
        scratch_shapes=[pltpu.SemaphoreType.DMA((4,))],
        compiler_params=params,
        name="place_first",
    )(place, own, near, below, above)
    input_grad = pl.pallas_call(
        last_kernel,
        out_shape=whole,
        in_specs=[SMEM, ANY] + [VMEM] * 2,
        out_specs=ANY,
        scratch_shapes=[pltpu.SemaphoreType.DMA((4,))],
        input_output_aliases={1: 0},
        compiler_params=params,
        name="place_last",
    )(place, first, beside, across)
    return (input_grad, down_grad)


def solution(mesh):
    zs = mesh.shape["dp"] // 4
    ys = mesh.shape["rep"] // 2
    finer = Mesh(mesh.devices.reshape(zs, 2, 2, ys, 2), (*DP, *REP))
    in_specs = (P(DP, REP), P(DP, REP), P(REP, None), P(None, REP), P(DP))
    out_specs = (P(DP, None), P(DP, REP))
    return jax.shard_map(
        on_device, mesh=finer, in_specs=in_specs, out_specs=out_specs, check_vma=False
    )
```

```python
import jax
import jax.numpy as jnp
from jax import lax
from jax.experimental import pallas as pl
from jax.experimental.pallas import tpu as pltpu
from jax.sharding import Mesh
from jax.sharding import PartitionSpec as P

DP = ("z", "xh", "core")
REP = ("y", "xl")
RING = ("xh", "xl")
NEAR = [(0, 1), (1, 0)]
FAR = [(0, 3), (3, 0), (1, 2), (2, 1)]
MIXED = [(i, i ^ 1 if i // 2 % 2 == 0 else i ^ 5) for i in range(8)]
ACROSS = [(0, 2), (2, 0), (1, 3), (3, 1)]
VMEM = pl.BlockSpec(memory_space=pltpu.VMEM)
SMEM = pl.BlockSpec(memory_space=pltpu.SMEM)
ANY = pl.BlockSpec(memory_space=pl.ANY)
LIMIT = 12 * 1024 * 1024


def dot(a, b):
    return jnp.dot(a, b, preferred_element_type=jnp.float32)


def split_kernel(place, whole, own, other):
    xl = place[2]
    part = own.shape[0] // 4
    for y in range(4):
        for x, out in ((xl, own), (1 - xl, other)):
            out[y * part:(y + 1) * part, :] = whole[pl.ds(pl.multiple_of((y * 2 + x) * part, 16), part), :]


def live_kernel(place, whole, own, other):
    xl, live = place[2], place[3]
    part = own.shape[0] // 4
    for y in range(4):
        for x, out in ((xl, own), (1 - xl, other)):
            first = pl.multiple_of((y * 2 + x) * part, 16)
            row = first + lax.broadcasted_iota(jnp.int32, (part, out.shape[1]), 0)
            out[y * part:(y + 1) * part, :] = jnp.where(row < live, whole[pl.ds(first, part), :], 0).astype(out.dtype)


def spread_kernel(place, own_set, near_set, out):
    xl = place[2]
    for y in range(out.shape[0]):
        out[y, xl] = own_set[...]
        out[y, 1 - xl] = near_set[...]


def own_kernel(grads, pre, down, out):
    blocks, _, features = grads.shape
    hidden = sum(dot(grads[j], down[j * features:(j + 1) * features, :]) for j in range(blocks))
    out[...] = jnp.where(pre[...] > 0, hidden, 0.0).astype(out.dtype)


def terms_kernel(place, grads, own, pre_far, down_mine, down_other, up_own, up_mine, up_other, terms, up_far):
    core = place[0]
    blocks, features = grads.shape[0], grads.shape[2]
    half = blocks // 2
    units = up_mine.shape[0]
    up_far[pl.ds(pl.multiple_of(core * units, 16), units), :] = up_mine[...]
    up_far[pl.ds(pl.multiple_of((1 - core) * units, 16), units), :] = up_other[...]
    far = sum(
        dot(grads[core * half + j], down_mine[j * features:(j + 1) * features, :]) for j in range(half)
    ) + sum(
        dot(grads[(1 - core) * half + j], down_other[j * features:(j + 1) * features, :]) for j in range(half)
    )
    far = jnp.where(pre_far[...] > 0, far, 0.0).astype(jnp.bfloat16)
    columns = terms.shape[1] // 4
    for i in range(4):
        at = slice(i * columns, (i + 1) * columns)
        terms[:, at] = (dot(own[...], up_own[:, at]) + dot(far, up_far[:, at])).astype(terms.dtype)


def down_kernel(place, grads, pre_own, pre_far, kept, sent):
    core, xh, xl, live = place[0], place[1], place[2], place[3]
    blocks, rows, features = grads.shape
    units = pre_own.shape[1]
    share = kept.shape[2]
    groups = features // (4 * share)
    at = lax.broadcasted_iota(jnp.int32, pre_own.shape, 0)
    part = rows // 4
    row = at + (at // part + xl) * part
    hidden = jnp.concatenate(
        [jnp.where(row < live, jnp.maximum(pre[...], 0), 0).astype(jnp.bfloat16) for pre in (pre_own, pre_far)],
        axis=1,
    )
    for j in range(blocks):
        block = lax.dot_general(
            grads[j], hidden, (((0,), (0,)), ((), ())), preferred_element_type=jnp.float32
        ).astype(kept.dtype)
        for g in range(groups):
            z = j * groups + g
            for h in range(2):
                first = (g * 4 + h * 2) * share
                low = block[first:first + share, :]
                high = block[first + share:first + 2 * share, :]
                mine = jnp.where(core == 0, low, high)
                other = jnp.where(core == 0, high, low)
                for t in range(2):
                    kind = t * 2 + jnp.abs(xh - h)
                    kept[kind, z] = mine[:, t * units:(t + 1) * units]
                    sent[kind, z] = other[:, t * units:(t + 1) * units]


def ring_kernel(own, near, far, across, out):
    total = own[...].astype(jnp.float32) + near[...].astype(jnp.float32)
    out[...] = (total + far[...].astype(jnp.float32) + across[...].astype(jnp.float32)).astype(out.dtype)


def put(place, blocks, out, sems):
    y, xl = place[4], place[2]
    rows = blocks[0][0].shape[0] if len(blocks[0]) == 3 else blocks[0][4]
    ranks = out.shape[0] // (2 * rows)
    running = []
    for i, (block, dy, dx, *rest) in enumerate(blocks):
        at = ((y + dy + ranks) % ranks) * 2 + (1 - xl if dx else xl)
        start = pl.multiple_of(at * rows, 16)
        for part in range(2):
            half = rows // 2
            source = block.at[pl.ds((rest[0] if rest else 0) + part * half, half)]
            copy = pltpu.make_async_copy(
                source, out.at[pl.ds(pl.multiple_of(start + part * half, 16), half)], sems.at[2 * i + part]
            )
            copy.start()
            running.append(copy)
    for copy in running:
        copy.wait()


def first_kernel(place, own, near, below, above, out, sems):
    put(place, [(own, 0, 0), (near, 0, 1), (below, -1, 0), (above, 1, 0)], out, sems)


def last_kernel(place, partial, beside, across, out, sems):
    rows = across.shape[0] // 2
    put(
        place,
        [(across, 2, 0, 0, rows), (across, 2, 1, rows, rows), (beside, -1, 1, 0, rows), (beside, 1, 1, rows, rows)],
        out,
        sems,
    )


def own_part(array, index, axis):
    return lax.dynamic_index_in_dim(array, index, axis, keepdims=False)


def on_device(grad_out, pre_act, up_weight, down_weight, slot_counts):
    slot_rows, features = grad_out.shape
    hidden_units = pre_act.shape[1]
    ys, zs = lax.axis_size("y"), lax.axis_size("z")
    reps = 2 * ys
    width = features * reps
    rows = slot_rows // reps
    half_rows = slot_rows // 2
    core, xh, xl, y = (lax.axis_index(a) for a in ("core", "xh", "xl", "y"))
    place = jnp.stack([core, xh, xl, slot_counts[0], y]).astype(jnp.int32)
    bf16 = jnp.bfloat16

    def turn(by):
        return [(i, (i + by) % ys) for i in range(ys)]

    params = pltpu.CompilerParams(vmem_limit_bytes=LIMIT)
    set_shape = jax.ShapeDtypeStruct((half_rows, features), bf16)
    pre_shape = jax.ShapeDtypeStruct((half_rows, hidden_units), bf16)
    own_set, other_set = pl.pallas_call(
        live_kernel,
        out_shape=(set_shape, set_shape),
        in_specs=[SMEM, VMEM],
        out_specs=(VMEM, VMEM),
        compiler_params=params,
        name="live_sets",
    )(place, grad_out)
    pre_own, pre_sent = pl.pallas_call(
        split_kernel,
        out_shape=(pre_shape, pre_shape),
        in_specs=[SMEM, VMEM],
        out_specs=(VMEM, VMEM),
        compiler_params=params,
        name="pre_sets",
    )(place, pre_act)
    near_set = lax.ppermute(other_set, "xl", NEAR)
    grads = pl.pallas_call(
        spread_kernel,
        out_shape=jax.ShapeDtypeStruct((ys, 2, half_rows, features), bf16),
        in_specs=[SMEM] + [VMEM] * 2,
        out_specs=VMEM,
        compiler_params=params,
        name="spread",
    )(place, own_set, near_set)
    grads = lax.all_to_all(grads, "y", 0, 0, tiled=True).reshape(reps, half_rows, features)
    pre_far = lax.ppermute(pre_sent, "xl", NEAR)

    down_mine = lax.ppermute(own_part(down_weight.reshape(2, width // 2, hidden_units), core, 0), RING, FAR)
    up_mine = lax.ppermute(
        own_part(up_weight.reshape(2, hidden_units // 2, width), core, 0), ("xh", "core", "xl"), MIXED
    )
    down_other = lax.ppermute(down_mine, "core", NEAR)
    up_other = lax.ppermute(up_mine, "core", NEAR)

    pre_grad = pl.pallas_call(
        own_kernel,
        out_shape=jax.ShapeDtypeStruct((half_rows, hidden_units), bf16),
        in_specs=[VMEM] * 3,
        out_specs=VMEM,
        compiler_params=pltpu.CompilerParams(vmem_limit_bytes=LIMIT),
        cost_estimate=pl.CostEstimate(
            flops=2 * half_rows * width * hidden_units, bytes_accessed=4 * width * hidden_units, transcendentals=0
        ),
        name="own_grad",
    )(grads, pre_own, down_weight)
    share = width // (4 * zs)
    laid_out = jax.ShapeDtypeStruct((4, zs, share, hidden_units), bf16)
    kept, sent = pl.pallas_call(
        down_kernel,
        out_shape=(laid_out, laid_out),
        in_specs=[SMEM] + [VMEM] * 3,
        out_specs=(VMEM, VMEM),
        compiler_params=pltpu.CompilerParams(vmem_limit_bytes=LIMIT),
        cost_estimate=pl.CostEstimate(
            flops=4 * half_rows * width * hidden_units, bytes_accessed=8 * width * hidden_units, transcendentals=0
        ),
        name="down_terms",
    )(place, grads, pre_own, pre_far)

    pre_later, sent = lax.optimization_barrier((pre_far, sent))
    terms = pl.pallas_call(
        terms_kernel,
        out_shape=jax.ShapeDtypeStruct((half_rows, width), bf16),
        in_specs=[SMEM] + [VMEM] * 8,
        out_specs=VMEM,
        scratch_shapes=[pltpu.VMEM((hidden_units, width), bf16)],
        compiler_params=pltpu.CompilerParams(vmem_limit_bytes=LIMIT),
        cost_estimate=pl.CostEstimate(
            flops=6 * half_rows * width * hidden_units, bytes_accessed=12 * width * hidden_units, transcendentals=0
        ),
        name="terms",
    )(place, grads, pre_grad, pre_later, down_mine, down_other, up_weight, up_mine, up_other)

    f32 = jnp.float32
    came = lax.all_to_all(terms.reshape(ys, rows, width), "y", 0, 0, tiled=True)
    own = sum(came[i].astype(f32) for i in range(ys)).astype(bf16)

    other = lax.ppermute(sent, "core", NEAR)
    chip = [(kept[k].astype(f32) + other[k].astype(f32)) for k in range(4)]
    ring = [
        lax.ppermute(chip[2].astype(bf16), "xl", NEAR),
        lax.ppermute(chip[3].astype(bf16), RING, FAR),
        lax.ppermute(chip[1].astype(bf16), RING, ACROSS),
    ]

    near = lax.ppermute(own, "xl", NEAR)
    below = lax.ppermute(own, "y", turn(1))
    above = lax.ppermute(own, "y", turn(-1))

    own_chip, ring, _ = lax.optimization_barrier((chip[0].astype(bf16), ring, own))
    ring_sum = pl.pallas_call(
        ring_kernel,
        out_shape=jax.ShapeDtypeStruct((zs, share, hidden_units), bf16),
        in_specs=[VMEM] * 4,
        out_specs=VMEM,
        compiler_params=params,
        cost_estimate=pl.CostEstimate(flops=2 * width * hidden_units, bytes_accessed=10 * width * hidden_units, transcendentals=0),
        name="ring_sum",
    )(own_chip, *ring)
    z_terms = lax.all_to_all(ring_sum, "z", 0, 0, tiled=True)
    down_grad = jnp.sum(z_terms.astype(f32), axis=0) / (4 * zs)

    near, below, above = lax.optimization_barrier((near, below, above))
    across = lax.ppermute(jnp.concatenate([own, near]), "y", turn(2))
    beside = lax.ppermute(jnp.concatenate([below, above]), "xl", NEAR)
    whole = jax.ShapeDtypeStruct((slot_rows, width), bf16)
    first = pl.pallas_call(
        first_kernel,
        out_shape=whole,
        in_specs=[SMEM] + [VMEM] * 4,
        out_specs=ANY,
        scratch_shapes=[pltpu.SemaphoreType.DMA((8,))],
        compiler_params=params,
        name="place_first",
    )(place, own, near, below, above)
    input_grad = pl.pallas_call(
        last_kernel,
        out_shape=whole,
        in_specs=[SMEM, ANY] + [VMEM] * 2,
        out_specs=ANY,
        scratch_shapes=[pltpu.SemaphoreType.DMA((8,))],
        input_output_aliases={1: 0},
        compiler_params=params,
        name="place_last",
    )(place, first, beside, across)
    return (input_grad, down_grad)


def solution(mesh):
    zs = mesh.shape["dp"] // 4
    ys = mesh.shape["rep"] // 2
    finer = Mesh(mesh.devices.reshape(zs, 2, 2, ys, 2), (*DP, *REP))
    in_specs = (P(DP, REP), P(DP, REP), P(REP, None), P(None, REP), P(DP))
    out_specs = (P(DP, None), P(DP, REP))
    return jax.shard_map(
        on_device, mesh=finer, in_specs=in_specs, out_specs=out_specs, check_vma=False
    )
```
